256 devices in a mesh: ang: 32 (over z, y), rad: 8 (over x, core).
Axes of the slice: x: 4, y: 4, z: 8, core: 2. Of those that a mesh axis runs over, the one named last changes fastest.
Arguments:
- field: bfloat16 [27, 128, 65536], P(None, 'rad', 'ang'), may hold values from -6 to 6
- velocity: bfloat16 [3, 128, 65536], P(None, 'rad', 'ang'), may hold values from -6 to 6
- send_cells: int32 [32, 32, 128], P('ang'), may hold values from 0 to 1791
- block_size: int32 [32, 32], P('ang'), may hold values from 0 to 128, as said below
- donor_slot: int32 [4, 8192], P(None, 'ang'), may hold values from 0 to 4095, as said below
- intersection_weight: float32 [4, 8192], P(None, 'ang'), may hold values from 0.05 to 0.6
- block_inverse: float32 [8, 16, 16], replicated
- lower_coupling: float32 [7], replicated, may hold values from -0.45 to -0.3
- upper_coupling: float32 [7], replicated, may hold values from -0.45 to -0.3
Outputs:
- solution: bfloat16 [27, 128, 65536], P(None, 'rad', 'ang')
The draws below stay inside these ranges and needn't reach their ends.
Inputs may be any that keep to these rules, and one draw needn't show every extreme that they name: `block_size`: only tiles of the other panel send to a tile: each tile receives live lists from 2 to 8 tiles of the other panel, at least one of them with all 128 slots live; one tile receives full lists from 8 tiles. `donor_slot`: every donor names a live slot, j < block_size[q, s]; the four donors of a ghost cell lie in one donor tile of its recipient or in two of them.
All inputs are finite; a program needn't handle non-finite values.
Results may differ from the reference program's by a relative error of at most 0.003.
Values may be sent and summed in bfloat16 or wider, within the bound.
No kernel may reach another device: no remote copies, remote signals or barrier semaphores. Data moves between devices by JAX's collectives and lax.ppermute only.
A program may use at most 128 MiB of HBM per device.

```python
import math
import jax
import jax.numpy as jnp
from jax import lax

C = 27
R_DEV = 16
A_DEV = 2048
TILES = 32
BLOCKS = 8
NR = 128
NA = 65536
RIM = 256
CAP = 128


def intersection_plan(key):
    keys = jax.random.split(jax.random.fold_in(key, 7), 7)
    half = TILES // 2
    tiles = jnp.arange(TILES, dtype=jnp.int32)
    hot = jax.random.randint(keys[0], (), 0, half)
    hot_count = min(8, half)
    counts = jnp.minimum(jax.random.randint(keys[1], (TILES,), 2, 5), half)
    counts = jnp.where(tiles == hot, hot_count, counts)
    start = jax.random.randint(keys[2], (TILES,), 0, half)
    start = jnp.where(tiles == hot, half - hot_count, start)
    start = jnp.where((tiles == 0) | (tiles == half), half - counts, start)
    start = jnp.where((tiles == half - 1) | (tiles == TILES - 1), 0, start)
    other_base = jnp.where(tiles < half, half, 0)
    sources = tiles[:, None]
    targets = tiles[None, :]
    in_other = sources // half != targets // half
    position = (sources - other_base[None, :]) % half
    rank = (position - start[None, :]) % half
    member = in_other & (rank < counts[None, :])
    sizes_drawn = jax.random.randint(keys[3], (TILES, TILES), CAP // 4, CAP + 1)
    forced = (sources == TILES - 1) & (targets == 0) | (sources == half - 1) & (targets == half)
    forced = forced | (sources == half) & (targets == half - 1) | (sources == 0) & (targets == TILES - 1)
    full = (rank == 0) | (targets == hot) | forced
    blocks_live = jnp.where(member, jnp.where(full, CAP, sizes_drawn), 0)
    recipient = jnp.arange(TILES * RIM, dtype=jnp.int32) // RIM
    own_count = counts[recipient]
    first_rank = jax.random.randint(keys[4], (TILES * RIM,), 0, 1 << 20) % (own_count - 1)
    step_up = jax.random.randint(keys[5], (4, TILES * RIM), 0, 2)
    ranks = first_rank[None, :] + step_up
    chosen = other_base[recipient][None, :] + (start[recipient][None, :] + ranks) % half
    counted = blocks_live[chosen, recipient[None, :]]
    slot = jax.random.randint(keys[6], (4, TILES * RIM), 0, 1 << 20) % counted
    plan = chosen * CAP + slot
    corner = jnp.arange(4, dtype=jnp.int32)
    hot_donor = other_base[hot] + start[hot] % half
    plan = plan.at[:, hot * RIM].set(hot_donor * CAP + CAP - 1 - corner)
    plan = plan.at[:, 1].set((TILES - 1) * CAP + CAP - 1 - corner)
    plan = plan.at[:, half * RIM].set((half - 1) * CAP + corner)
    plan = plan.at[:, (half - 1) * RIM + 1].set(half * CAP + corner)
    plan = plan.at[:, (TILES - 1) * RIM + 1].set(corner)
    return (blocks_live.astype(jnp.int32), plan.astype(jnp.int32))


def draw_block_size(key, part):
    return intersection_plan(key)[0]


def draw_donor_slot(key, part):
    return intersection_plan(key)[1]


def draw_block_inverse(key, part):
    keys = jax.random.split(jax.random.fold_in(key, 11), 3)
    rows = jnp.arange(R_DEV)
    spread = jax.random.uniform(keys[0], (BLOCKS, R_DEV, R_DEV), jnp.float32, -1.0, 1.0) * (0.4 / math.sqrt(R_DEV))
    edge = jnp.where((rows == 0) | (rows == R_DEV - 1), 2.0, 1.0)
    offdiag = (rows[:, None] != rows[None, :]).astype(jnp.float32)
    spread = spread * edge[None, None, :] * offdiag[None]
    corner_mask = ((rows[:, None] == 0) & (rows[None, :] == R_DEV - 1) | (rows[:, None] == R_DEV - 1) & (rows[None, :] == 0)).astype(jnp.float32)
    main = jax.random.uniform(keys[1], (BLOCKS, R_DEV), jnp.float32, 0.8, 1.2)
    corners = jax.random.uniform(keys[2], (BLOCKS, R_DEV, R_DEV), jnp.float32, 0.5, 0.7)
    spread = spread * (1.0 - corner_mask[None]) + corners * corner_mask[None]
    return spread + main[:, :, None] * jnp.eye(R_DEV, dtype=jnp.float32)[None]


def set_ends(drawn, rng, smallest, top_value):
    index_at = [jax.random.randint(jax.random.fold_in(rng, axis), (), 0, length) for axis, length in enumerate(drawn.shape)]
    widest = drawn.shape.index(max(drawn.shape))
    neighbour = index_at[:widest] + [(index_at[widest] + 1) % drawn.shape[widest]] + index_at[widest + 1:]
    return drawn.at[tuple(index_at)].set(smallest).at[tuple(neighbour)].set(top_value)


def block_levels(own_key, extent, shards, low, high):
    factor_of, own = 1.0, jax.random.fold_in(own_key, 6)
    for dim, blocks in shards:
        heights = jnp.exp(jax.random.uniform(jax.random.fold_in(own, dim), (blocks,), jnp.float32, low / len(shards), high / len(shards)))
        factor_of = factor_of * jnp.repeat(heights, extent[dim] // blocks).reshape([-1 if axis == dim else 1 for axis in range(len(extent))])
    return factor_of


def gaussian(own_key, shape, deviation, limit, cuts=(), held_as=jnp.bfloat16):
    entries = jax.random.normal(own_key, shape, jnp.float32) * deviation
    if len(cuts) > 0:
        entries = block_levels(own_key, shape, cuts, -0.22, 0.18) * entries
    return jnp.clip(entries, min=-limit, max=limit).astype(held_as)


def setup_inputs(seed: int = 0) -> dict:
    key_list = jax.random.split(jax.random.key(seed), 10)
    return {
        "field": gaussian(key_list[0], (C, NR, NA), 1.0, 6.0, ((1, 8), (2, 32))),
        "velocity": gaussian(key_list[1], (3, NR, NA), 1.0, 6.0, ((1, 8), (2, 32))),
        "send_cells": set_ends(jax.random.randint(key_list[2], (TILES, TILES, CAP), 0, A_DEV - RIM), jax.random.fold_in(key_list[2], 1), 0, (A_DEV - RIM) - 1).astype(jnp.int32),
        "block_size": draw_block_size(jax.random.fold_in(key_list[9], 71), 0),
        "donor_slot": draw_donor_slot(jax.random.fold_in(key_list[9], 71), 0),
        "intersection_weight": jnp.clip(0.05 + 0.55 * jax.random.uniform(key_list[5], (4, NA // 8), jnp.float32) ** block_levels(key_list[5], (4, NA // 8), ((1, 32),), -0.2, 0.2), 0.05, 0.6),
        "block_inverse": draw_block_inverse(jax.random.fold_in(key_list[9], 71), 0),
        "lower_coupling": jnp.clip(jax.random.uniform(key_list[7], (BLOCKS - 1,), jnp.float32, -0.45, -0.3), -0.45, -0.3),
        "upper_coupling": jnp.clip(jax.random.uniform(key_list[8], (BLOCKS - 1,), jnp.float32, -0.45, -0.3), -0.45, -0.3),
    }


induction = 0.5

def cross_source(field, velocity):
    shape = field.shape
    groups = field.reshape((shape[0] // 3, 3) + shape[1:])
    first = velocity[1] * groups[:, 2] - velocity[2] * groups[:, 1]
    second = velocity[2] * groups[:, 0] - velocity[0] * groups[:, 2]
    third = velocity[0] * groups[:, 1] - velocity[1] * groups[:, 0]
    crossed = jnp.stack([first, second, third], axis=1).reshape(shape)
    return field + induction * crossed

def alternate(even_part, odd_part):
    return jnp.stack([even_part, odd_part], axis=1).reshape(-1)

def interface_matrix(block_inverse, lower_coupling, upper_coupling):
    blocks = block_inverse.shape[0]
    nothing = jnp.zeros((1,), jnp.float32)
    upper = jnp.concatenate([upper_coupling, nothing])
    lower = jnp.concatenate([nothing, lower_coupling])
    right = block_inverse[:, :, -1] * upper[:, None]
    left = block_inverse[:, :, 0] * lower[:, None]
    zero_vector = jnp.zeros((blocks,), jnp.float32)
    size = 2 * blocks
    ahead_two = alternate(right[:, 0], zero_vector)
    ahead_one = alternate(zero_vector, right[:, -1])
    behind_one = alternate(left[:, 0], zero_vector)
    behind_two = alternate(zero_vector, left[:, -1])
    matrix = jnp.eye(size, dtype=jnp.float32)
    matrix = matrix + jnp.diag(ahead_two[:size - 2], 2) + jnp.diag(ahead_one[:size - 1], 1)
    matrix = matrix + jnp.diag(behind_one[1:], -1) + jnp.diag(behind_two[2:], -2)
    return (matrix, right, left)

def reference(field, velocity, send_cells, block_size, donor_slot, intersection_weight, block_inverse, lower_coupling, upper_coupling):
    channels, radii, cells_all = field.shape
    tile_count = send_cells.shape[0]
    capacity = send_cells.shape[2]
    tile_cells = cells_all // tile_count
    ghosts = donor_slot.shape[1] // tile_count
    inner = tile_cells - ghosts
    blocks, block_depth, _ = block_inverse.shape
    matrix, right, left = interface_matrix(block_inverse, lower_coupling, upper_coupling)
    offsets = jnp.arange(tile_count, dtype=jnp.int32) * tile_cells
    flat_cells = send_cells + offsets[:, None, None]
    live = jnp.arange(capacity, dtype=jnp.int32)[None, None, :] < block_size[:, :, None]

    def one_tile(recipient):
        cells = flat_cells[:, recipient, :].reshape(-1)
        mask = live[:, recipient, :].reshape(-1)
        donors = cross_source(jnp.take(field, cells, axis=2).astype(jnp.float32), jnp.take(velocity, cells, axis=2).astype(jnp.float32))
        donors = jnp.where(mask[None, None, :], donors, 0.0)
        slots = lax.dynamic_slice_in_dim(donor_slot, (recipient * ghosts).astype(jnp.int32), ghosts, 1)
        weights = lax.dynamic_slice_in_dim(intersection_weight, (recipient * ghosts).astype(jnp.int32), ghosts, 1)
        picked = jnp.take(donors, slots.reshape(-1), axis=2).reshape(channels, radii, 4, ghosts)
        ghost = jnp.sum(picked * weights[None, None], axis=2)
        own_field = lax.dynamic_slice_in_dim(field, (recipient * tile_cells).astype(jnp.int32), tile_cells, 2)
        own_flow = lax.dynamic_slice_in_dim(velocity, (recipient * tile_cells).astype(jnp.int32), tile_cells, 2)
        interior = cross_source(own_field[:, :, :inner].astype(jnp.float32), own_flow[:, :, :inner].astype(jnp.float32))
        filled = jnp.concatenate([interior, ghost], axis=2)
        spread = jnp.einsum('kij,ckja->ckia', block_inverse, filled.reshape(channels, blocks, block_depth, tile_cells), precision=lax.Precision.HIGHEST)
        edges = jnp.stack([spread[:, :, 0, :], spread[:, :, -1, :]], axis=2)
        edges = edges.transpose(1, 2, 0, 3).reshape(2 * blocks, channels * tile_cells)
        values = jnp.linalg.solve(matrix, edges).reshape(blocks, 2, channels, tile_cells)
        nothing = jnp.zeros((1, channels, tile_cells), jnp.float32)
        top_next = jnp.concatenate([values[1:, 0], nothing], axis=0).transpose(1, 0, 2)[:, :, None, :]
        bottom_prev = jnp.concatenate([nothing, values[:-1, 1]], axis=0).transpose(1, 0, 2)[:, :, None, :]
        result = spread - right[None, :, :, None] * top_next - left[None, :, :, None] * bottom_prev
        return result.reshape(channels, radii, tile_cells).astype(jnp.bfloat16)
    stacked = lax.map(one_tile, jnp.arange(tile_count, dtype=jnp.int32))
    return stacked.transpose(1, 2, 0, 3).reshape(channels, radii, cells_all)
```

```python
import jax
import jax.numpy as jnp
from jax import lax
from jax.experimental import pallas as pl
from jax.experimental.pallas import tpu as pltpu
from jax.sharding import PartitionSpec as P

f32 = jnp.float32
bf16 = jnp.bfloat16
highest = lax.Precision.HIGHEST
induction = 0.5

CHANNELS = 27
DEPTH = 16
ROWS = CHANNELS * DEPTH
CELLS = 2048
RIM = 256
INNER = CELLS - RIM
CAP = 128
TILES = 32
BLOCKS = 8
PARTS = 3
PART_ROWS = ROWS // PARTS
EDGE = 64
GROUP = 8
VMEM_LIMIT = 48 * 1024 * 1024

SERVES = ((3, 1, 2, 0), (2, 0, 3, 1))


def params():
    return pltpu.CompilerParams(vmem_limit_bytes=VMEM_LIMIT)


def iota(shape, axis):
    return lax.broadcasted_iota(jnp.int32, shape, axis)


def split(value):
    high = value.astype(bf16)
    return high, (value - high.astype(f32)).astype(bf16)


def dot(left, right):
    return jnp.dot(left, right, preferred_element_type=f32)


def spread_kernel(place, field, velocity, block_inverse, spread, rounded, high_mat, low_mat):
    @pl.when(pl.program_id(0) == 0)
    def _():
        own = block_inverse[place[1]]
        size = PART_ROWS
        rows = (iota((size, DEPTH), 0) % DEPTH == iota((size, DEPTH), 1)).astype(f32)
        columns = (iota((DEPTH, size), 1) % DEPTH == iota((DEPTH, size), 0)).astype(f32)
        tiled = jnp.dot(jnp.dot(rows, own, precision=highest), columns, precision=highest)
        same = iota((size, size), 0) // DEPTH == iota((size, size), 1) // DEPTH
        high, low = split(jnp.where(same, tiled, 0.0))
        high_mat[...] = high
        low_mat[...] = low

    flow = [velocity[DEPTH * i : DEPTH * (i + 1), :INNER].astype(f32) for i in range(3)]
    parts = []
    for m in range(PART_ROWS // (3 * DEPTH)):
        f = [
            field[DEPTH * (3 * m + i) : DEPTH * (3 * m + i + 1), :INNER].astype(f32)
            for i in range(3)
        ]
        for i in range(3):
            j, k = (i + 1) % 3, (i + 2) % 3
            parts.append(f[i] + induction * (flow[j] * f[k] - flow[k] * f[j]))
    source_high, source_low = split(jnp.concatenate(parts, axis=0))
    result = dot(high_mat[...], source_high) + dot(high_mat[...], source_low)
    result = result + dot(low_mat[...], source_high)
    spread[...] = result
    rounded[...] = result.astype(bf16)


def edge_select():
    row, column = iota((EDGE, ROWS), 0), iota((EDGE, ROWS), 1)
    wanted = (row % 32) * DEPTH + (row // 32) * (DEPTH - 1)
    return ((row % 32 < CHANNELS) & (column == wanted)).astype(f32).astype(bf16)


def list_kernel(place, block_size, cells, rounded, lists, edges):
    step = pl.program_id(0)
    row = place[0] // 4
    panel, half = row // 4, (row // 2) % 2
    member, y = step // 4, step % 4
    served = (3 - 2 * member - half, 2 - 2 * member + half)
    wanted = []
    for m in range(2):
        tile = (4 * (1 - panel) + served[m]) * 4 + y
        listed = cells[0, pl.ds(tile, 1), :]
        wanted.append(jnp.where(iota((1, CAP), 1) < block_size[0, tile], listed, -1))
    wanted = jnp.concatenate(wanted, axis=1)
    total = jnp.zeros((ROWS, 2 * CAP), f32)
    for first in range(0, INNER, 256):
        hot = (iota((256, 2 * CAP), 0) + first == wanted).astype(f32).astype(bf16)
        total = total + dot(rounded[:, first : first + 256], hot)
    lists[0] = total.astype(bf16)

    start = pl.multiple_of(jnp.minimum(step, INNER // 256 - 1) * 256, 256)
    edges[0] = dot(edge_select(), rounded[:, pl.ds(start, 256)]).astype(bf16)


def weight_kernel(place, first, second, weights):
    base = (place[0] // GROUP) * (GROUP * CAP)
    for m, meta in enumerate((first, second)):
        slots = meta[0:4, :].astype(jnp.int32) - base
        for t in range(GROUP):
            position = iota((CAP, RIM), 0) + t * CAP
            value = jnp.zeros((CAP, RIM), f32)
            for d in range(4):
                value = value + jnp.where(slots[d : d + 1, :] == position, meta[4 + d : 5 + d, :], 0.0)
            high, low = split(value)
            weights[m, t * CAP : (t + 1) * CAP, :RIM] = high
            weights[m, t * CAP : (t + 1) * CAP, RIM:] = low


def setup_kernel(place, lower, upper, corner, block_inverse, needed, spikes):
    size = 2 * BLOCKS
    shape = (size, 128)
    row, lane = iota(shape, 0), iota(shape, 1)
    work = ((row == lane) | (row + size == lane)).astype(f32)
    for k in range(BLOCKS):
        for b in range(2):
            i = b * (DEPTH - 1)
            here = row == 2 * k + b
            if k < BLOCKS - 1:
                value = corner[k, i, DEPTH - 1] * upper[k]
                work = jnp.where(here & (lane == 2 * k + 2), value, work)
            if k > 0:
                value = corner[k, i, 0] * lower[k - 1]
                work = jnp.where(here & (lane == 2 * k - 1), value, work)
    for p in range(size):
        column = jnp.sum(jnp.where(lane == p, work, 0.0), axis=1, keepdims=True)
        chosen = work[p : p + 1, :] / column[p : p + 1, :]
        work = jnp.where(row == p, chosen, work - column * chosen)
    up = jnp.concatenate([work[2:, :], jnp.zeros((2, 128), f32)], axis=0)
    down = jnp.concatenate([jnp.zeros((2, 128), f32), work[:-2, :]], axis=0)
    needed[...] = jnp.where(row % 2 == 0, up, down)

    k = place[1]
    ahead = jnp.where(k < BLOCKS - 1, upper[jnp.minimum(k, BLOCKS - 2)], 0.0)
    behind = jnp.where(k > 0, lower[jnp.maximum(k - 1, 0)], 0.0)
    rows = (iota((ROWS, DEPTH), 0) % DEPTH == iota((ROWS, DEPTH), 1)).astype(f32)
    tiled = jnp.dot(rows, block_inverse[k], precision=highest)
    right, left = tiled[:, DEPTH - 1 :] * ahead, tiled[:, :1] * behind
    channel, lane = iota((ROWS, 128), 0) // DEPTH, iota((ROWS, 128), 1)
    full = jnp.where(lane % 64 == channel, right, 0.0)
    full = full + jnp.where(lane % 64 == channel + 32, left, 0.0)
    high, low = split(full)
    spikes[...] = jnp.where(lane < 64, high.astype(f32), low.astype(f32)).astype(bf16)


def partial_kernel(lists, weights, first, second, first_edges, second_edges):
    for m, (partial, edges) in enumerate(((first, first_edges), (second, second_edges))):
        values = [lists[t, :, m * CAP : (m + 1) * CAP] for t in range(GROUP)]
        both = dot(jnp.concatenate(values, axis=1), weights[m])
        result = (both[:, :RIM] + both[:, RIM:]).astype(bf16)
        partial[...] = result
        edges[...] = dot(edge_select(), result).astype(bf16)


def join_kernel(whole, first, second, edges):
    edges[0] = (first[...].astype(f32) + second[...].astype(f32)).astype(bf16)


def solve_kernel(needed, edges, coupled):
    values = []
    for k in range(BLOCKS):
        for b in range(2):
            values.append(edges[k, 32 * b : 32 * b + 32, :].astype(f32))
    for k in range(BLOCKS):
        for b in range(2):
            total = needed[2 * k + b, 2 * BLOCKS] * values[0]
            for q in range(1, 2 * BLOCKS):
                total = total + needed[2 * k + b, 2 * BLOCKS + q] * values[q]
            coupled[k, 32 * b : 32 * b + 32, :] = total.astype(bf16)


def finish_kernel(spread, first, second, spikes, coupled, result):
    twice = jnp.concatenate([coupled[0], coupled[0]], axis=0)
    correction = dot(spikes[...], twice)

    @pl.when(pl.program_id(0) < INNER // 256)
    def _():
        result[...] = (spread[...] - correction).astype(bf16)

    @pl.when(pl.program_id(0) == INNER // 256)
    def _():
        ghost = first[...].astype(f32) + second[...].astype(f32)
        result[...] = (ghost - correction).astype(bf16)


SMEM = pl.BlockSpec(memory_space=pltpu.SMEM)


def whole(shape):
    return pl.BlockSpec(shape, lambda i: (0,) * len(shape))


def crossing(m, backwards):
    pairs = []
    for z in range(8):
        panel, i = divmod(z, 4)
        target = 4 * (1 - panel) + SERVES[m][i]
        for y in range(4):
            pair = (z * 4 + y, target * 4 + y)
            pairs.append(pair[::-1] if backwards else pair)
    return pairs


def shards(
    field,
    velocity,
    send_cells,
    block_size,
    donor_slot,
    intersection_weight,
    block_inverse,
    lower_coupling,
    upper_coupling,
):
    field = field.reshape(ROWS, CELLS)
    velocity = velocity.reshape(3 * DEPTH, CELLS)
    place = jnp.stack([lax.axis_index("ang"), lax.axis_index("rad")]).astype(jnp.int32)
    groups = [list(range(g * GROUP, (g + 1) * GROUP)) for g in range(TILES // GROUP)]

    meta = jnp.concatenate([donor_slot.astype(f32), intersection_weight], axis=0)
    metas = [lax.ppermute(meta, "ang", crossing(m, True)) for m in range(2)]

    spread, rounded = pl.pallas_call(
        spread_kernel,
        grid=(PARTS,),
        in_specs=[
            SMEM,
            pl.BlockSpec((PART_ROWS, CELLS), lambda i: (i, 0)),
            whole((3 * DEPTH, CELLS)),
            whole((BLOCKS, DEPTH, DEPTH)),
        ],
        out_specs=[
            pl.BlockSpec((PART_ROWS, INNER), lambda i: (i, 0)),
            pl.BlockSpec((PART_ROWS, INNER), lambda i: (i, 0)),
        ],
        out_shape=[
            jax.ShapeDtypeStruct((ROWS, INNER), f32),
            jax.ShapeDtypeStruct((ROWS, INNER), bf16),
        ],
        scratch_shapes=[pltpu.VMEM((PART_ROWS, PART_ROWS), bf16)] * 2,
        compiler_params=params(),
        name="spread",
    )(place, field, velocity, block_inverse)

    lists, edges = pl.pallas_call(
        list_kernel,
        grid=(GROUP,),
        in_specs=[SMEM, SMEM, whole((1, TILES, CAP)), whole((ROWS, INNER))],
        out_specs=[
            pl.BlockSpec((1, ROWS, 2 * CAP), lambda i: (i, 0, 0)),
            pl.BlockSpec((1, EDGE, 256), lambda i: (i, 0, 0)),
        ],
        out_shape=[
            jax.ShapeDtypeStruct((GROUP, ROWS, 2 * CAP), bf16),
            jax.ShapeDtypeStruct((GROUP, EDGE, 256), bf16),
        ],
        compiler_params=params(),
        name="lists",
    )(place, block_size, send_cells, rounded)

    donors = lax.all_to_all(lists, "ang", 0, 0, axis_index_groups=groups)

    weights = pl.pallas_call(
        weight_kernel,
        in_specs=[SMEM, pl.BlockSpec(memory_space=pltpu.VMEM), pl.BlockSpec(memory_space=pltpu.VMEM)],
        out_specs=pl.BlockSpec(memory_space=pltpu.VMEM),
        out_shape=jax.ShapeDtypeStruct((2, GROUP * CAP, 2 * RIM), bf16),
        compiler_params=params(),
        name="weights",
    )(place, *metas)

    needed, spikes = pl.pallas_call(
        setup_kernel,
        in_specs=[SMEM, SMEM, SMEM, SMEM, pl.BlockSpec(memory_space=pltpu.VMEM)],
        out_specs=[pl.BlockSpec(memory_space=pltpu.VMEM)] * 2,
        out_shape=[
            jax.ShapeDtypeStruct((2 * BLOCKS, 128), f32),
            jax.ShapeDtypeStruct((ROWS, 128), bf16),
        ],
        compiler_params=params(),
        name="setup",
    )(place, lower_coupling, upper_coupling, block_inverse, block_inverse)

    outs = pl.pallas_call(
        partial_kernel,
        in_specs=[pl.BlockSpec(memory_space=pltpu.VMEM)] * 2,
        out_specs=[pl.BlockSpec(memory_space=pltpu.VMEM)] * 4,
        out_shape=[jax.ShapeDtypeStruct((ROWS, RIM), bf16)] * 2
        + [jax.ShapeDtypeStruct((EDGE, RIM), bf16)] * 2,
        compiler_params=params(),
        name="partial",
    )(donors, weights)

    ghost_edges = [lax.ppermute(outs[2 + m], "ang", crossing(m, False)) for m in range(2)]
    ghosts = [lax.ppermute(outs[m], "ang", crossing(m, False)) for m in range(2)]

    edges = pl.pallas_call(
        join_kernel,
        grid=(1,),
        in_specs=[pl.BlockSpec(memory_space=pl.ANY), whole((EDGE, RIM)), whole((EDGE, RIM))],
        out_specs=pl.BlockSpec((1, EDGE, 256), lambda i: (GROUP - 1, 0, 0)),
        out_shape=jax.ShapeDtypeStruct((GROUP, EDGE, 256), bf16),
        input_output_aliases={0: 0},
        compiler_params=params(),
        name="join",
    )(edges, *ghost_edges)

    edges = lax.all_to_all(edges, "rad", 0, 0)
    coupled = pl.pallas_call(
        solve_kernel,
        in_specs=[SMEM, pl.BlockSpec(memory_space=pltpu.VMEM)],
        out_specs=pl.BlockSpec(memory_space=pltpu.VMEM),
        out_shape=jax.ShapeDtypeStruct((BLOCKS, EDGE, 256), bf16),
        compiler_params=params(),
        name="solve",
    )(needed, edges)
    coupled = lax.all_to_all(coupled, "rad", 0, 0)

    result = pl.pallas_call(
        finish_kernel,
        grid=(CELLS // 256,),
        in_specs=[
            pl.BlockSpec((ROWS, 256), lambda i: (0, jnp.minimum(i, INNER // 256 - 1))),
            whole((ROWS, RIM)),
            whole((ROWS, RIM)),
            whole((ROWS, 128)),
            pl.BlockSpec((1, EDGE, 256), lambda i: (i, 0, 0)),
        ],
        out_specs=pl.BlockSpec((ROWS, 256), lambda i: (0, i)),
        out_shape=jax.ShapeDtypeStruct((ROWS, CELLS), bf16),
        compiler_params=params(),
        name="finish",
    )(spread, *ghosts, spikes, coupled)
    return result.reshape(CHANNELS, DEPTH, CELLS)


def solution(mesh):
    in_specs = (
        P(None, "rad", "ang"),
        P(None, "rad", "ang"),
        P("ang", None, None),
        P("ang", None),
        P(None, "ang"),
        P(None, "ang"),
        P(),
        P(),
        P(),
    )
    out_specs = P(None, "rad", "ang")
    return jax.shard_map(shards, mesh=mesh, in_specs=in_specs, out_specs=out_specs, check_vma=False)
```

```python
import jax
import jax.numpy as jnp
from jax import lax
from jax.experimental import pallas as pl
from jax.experimental.pallas import tpu as pltpu
from jax.sharding import PartitionSpec as P

f32 = jnp.float32
bf16 = jnp.bfloat16
highest = lax.Precision.HIGHEST
induction = 0.5

CHANNELS = 27
DEPTH = 16
ROWS = CHANNELS * DEPTH
CELLS = 2048
RIM = 256
INNER = CELLS - RIM
CAP = 128
TILES = 32
BLOCKS = 8
PARTS = 3
PART_ROWS = ROWS // PARTS
EDGE = 64
GROUP = 8
EARLY = 160

SERVES = ((3, 1, 2, 0), (2, 0, 3, 1))


def params(mebibytes):
    return pltpu.CompilerParams(vmem_limit_bytes=mebibytes * 1024 * 1024)


def iota(shape, axis):
    return lax.broadcasted_iota(jnp.int32, shape, axis)


def split(value):
    high = value.astype(bf16)
    return high, (value - high.astype(f32)).astype(bf16)


def dot(left, right):
    return jnp.dot(left, right, preferred_element_type=f32)


def spread_kernel(place, field, velocity, block_inverse, spread, rounded, high_mat, low_mat):
    @pl.when(pl.program_id(0) == 0)
    def _():
        own = block_inverse[place[1]]
        size = PART_ROWS
        rows = (iota((size, DEPTH), 0) % DEPTH == iota((size, DEPTH), 1)).astype(f32)
        columns = (iota((DEPTH, size), 1) % DEPTH == iota((DEPTH, size), 0)).astype(f32)
        tiled = jnp.dot(jnp.dot(rows, own, precision=highest), columns, precision=highest)
        same = iota((size, size), 0) // DEPTH == iota((size, size), 1) // DEPTH
        high, low = split(jnp.where(same, tiled, 0.0))
        high_mat[...] = high
        low_mat[...] = low

    flow = [velocity[DEPTH * i : DEPTH * (i + 1), :INNER].astype(f32) for i in range(3)]
    parts = []
    for m in range(PART_ROWS // (3 * DEPTH)):
        f = [
            field[DEPTH * (3 * m + i) : DEPTH * (3 * m + i + 1), :INNER].astype(f32)
            for i in range(3)
        ]
        for i in range(3):
            j, k = (i + 1) % 3, (i + 2) % 3
            parts.append(f[i] + induction * (flow[j] * f[k] - flow[k] * f[j]))
    source_high, source_low = split(jnp.concatenate(parts, axis=0))
    result = dot(high_mat[...], source_high) + dot(high_mat[...], source_low)
    result = result + dot(low_mat[...], source_high)
    spread[...] = result
    rounded[...] = result.astype(bf16)


def edge_select():
    row, column = iota((EDGE, ROWS), 0), iota((EDGE, ROWS), 1)
    wanted = (row % 32) * DEPTH + (row // 32) * (DEPTH - 1)
    return ((row % 32 < CHANNELS) & (column == wanted)).astype(f32).astype(bf16)


def list_kernel(place, block_size, cells, rounded, *outs):
    row, y = place[0] // 4, place[0] % 4
    panel, half = row // 4, (row // 2) % 2
    for r in range(GROUP):
        member = (row + r // 4) % 2
        served = (3 - 2 * member - half, 2 - 2 * member + half)
        wanted = []
        for m in range(2):
            tile = (4 * (1 - panel) + served[m]) * 4 + (y + r) % 4
            listed = cells[0, pl.ds(tile, 1), :]
            wanted.append(jnp.where(iota((1, CAP), 1) < block_size[0, tile], listed, -1))
        wanted = jnp.concatenate(wanted, axis=1)
        total = jnp.zeros((ROWS, 2 * CAP), f32)
        for first in range(0, INNER, 256):
            hot = (iota((256, 2 * CAP), 0) + first == wanted).astype(f32).astype(bf16)
            total = total + dot(rounded[:, first : first + 256], hot)
        outs[r][...] = total.astype(bf16)

    for j in range(BLOCKS):
        first = min(j, INNER // 256 - 1) * 256
        outs[GROUP][j] = dot(edge_select(), rounded[:, first : first + 256]).astype(bf16)


def weight_kernel(place, first, second, weights):
    row, y = place[0] // 4, place[0] % 4
    for m, meta in enumerate((first, second)):
        slots = meta[0:4, :].astype(jnp.int32)
        for r in range(GROUP):
            tile = (row // 2 * 2 + (row + r // 4) % 2) * 4 + (y + 4 - r % 4) % 4
            position = iota((CAP, RIM), 0) + tile * CAP
            value = jnp.zeros((CAP, RIM), f32)
            for d in range(4):
                value = value + jnp.where(slots[d : d + 1, :] == position, meta[4 + d : 5 + d, :], 0.0)
            high, low = split(value)
            weights[m, r * CAP : (r + 1) * CAP, :RIM] = high
            weights[m, r * CAP : (r + 1) * CAP, RIM:] = low


def setup_kernel(place, lower, upper, corner, block_inverse, needed, spikes):
    size = 2 * BLOCKS
    shape = (size, 128)
    row, lane = iota(shape, 0), iota(shape, 1)
    work = ((row == lane) | (row + size == lane)).astype(f32)
    for k in range(BLOCKS):
        for b in range(2):
            i = b * (DEPTH - 1)
            here = row == 2 * k + b
            if k < BLOCKS - 1:
                value = corner[k, i, DEPTH - 1] * upper[k]
                work = jnp.where(here & (lane == 2 * k + 2), value, work)
            if k > 0:
                value = corner[k, i, 0] * lower[k - 1]
                work = jnp.where(here & (lane == 2 * k - 1), value, work)
    for p in range(size):
        column = jnp.sum(jnp.where(lane == p, work, 0.0), axis=1, keepdims=True)
        chosen = work[p : p + 1, :] / column[p : p + 1, :]
        work = jnp.where(row == p, chosen, work - column * chosen)
    up = jnp.concatenate([work[2:, :], jnp.zeros((2, 128), f32)], axis=0)
    down = jnp.concatenate([jnp.zeros((2, 128), f32), work[:-2, :]], axis=0)
    needed[...] = jnp.where(row % 2 == 0, up, down)

    k = place[1]
    ahead = jnp.where(k < BLOCKS - 1, upper[jnp.minimum(k, BLOCKS - 2)], 0.0)
    behind = jnp.where(k > 0, lower[jnp.maximum(k - 1, 0)], 0.0)
    rows = (iota((ROWS, DEPTH), 0) % DEPTH == iota((ROWS, DEPTH), 1)).astype(f32)
    tiled = jnp.dot(rows, block_inverse[k], precision=highest)
    right, left = tiled[:, DEPTH - 1 :] * ahead, tiled[:, :1] * behind
    channel, lane = iota((ROWS, 128), 0) // DEPTH, iota((ROWS, 128), 1)
    full = jnp.where(lane % 64 == channel, right, 0.0)
    full = full + jnp.where(lane % 64 == channel + 32, left, 0.0)
    high, low = split(full)
    spikes[...] = jnp.where(lane < 64, high.astype(f32), low.astype(f32)).astype(bf16)


def partial_kernel(weights, *refs):
    lists, outs = refs[:GROUP], refs[GROUP:]
    for m in range(2):
        values = [lists[r][:, m * CAP : (m + 1) * CAP] for r in range(GROUP)]
        both = dot(jnp.concatenate(values, axis=1), weights[m])
        result = (both[:, :RIM] + both[:, RIM:]).astype(bf16)
        outs[m][:EDGE, :] = dot(edge_select(), result).astype(bf16)
        outs[m][EDGE:, :] = result[:EARLY, :]
        outs[2 + m][...] = result[EARLY:, :]


def join_kernel(first, second, edges):
    edges[...] = (first[:EDGE, :].astype(f32) + second[:EDGE, :].astype(f32)).astype(bf16)


def solve_kernel(needed, edges, coupled):
    values = []
    for k in range(BLOCKS):
        for b in range(2):
            values.append(edges[k, 32 * b : 32 * b + 32, :].astype(f32))
    for k in range(BLOCKS):
        for b in range(2):
            total = needed[2 * k + b, 2 * BLOCKS] * values[0]
            for q in range(1, 2 * BLOCKS):
                total = total + needed[2 * k + b, 2 * BLOCKS + q] * values[q]
            coupled[k, 32 * b : 32 * b + 32, :] = total.astype(bf16)


def finish_kernel(spread, spikes, coupled, result):
    twice = jnp.concatenate([coupled[0], coupled[0]], axis=0)
    result[...] = (spread[...] - dot(spikes[...], twice)).astype(bf16)


def ghost_kernel(place, needed, whole, *refs):
    del whole
    early, late, edges, (spikes, result) = refs[:2], refs[2:4], refs[4:12], refs[12:]
    own = place[1]
    halves = []
    for p in range(2):
        total = jnp.zeros((32, RIM), f32)
        for shift in range(BLOCKS):
            k = (own + BLOCKS - shift) % BLOCKS
            for b in range(2):
                factor = needed[2 * own + p, 2 * BLOCKS + 2 * k + b]
                total = total + factor * edges[shift][32 * b : 32 * b + 32, :].astype(f32)
        halves.append(total)
    high, low = split(jnp.concatenate(halves, axis=0))
    both = jnp.concatenate([high, high], axis=0)
    correction = dot(spikes[...], both) + dot(spikes[:, :EDGE], low)
    ghost = early[0][EDGE:, :].astype(f32) + early[1][EDGE:, :].astype(f32)
    result[:EARLY, :] = (ghost - correction[:EARLY, :]).astype(bf16)
    ghost = late[0][...].astype(f32) + late[1][...].astype(f32)
    result[EARLY:, :] = (ghost - correction[EARLY:, :]).astype(bf16)


SMEM = pl.BlockSpec(memory_space=pltpu.SMEM)


def whole(shape):
    return pl.BlockSpec(shape, lambda i: (0,) * len(shape))


def crossing(m, backwards):
    pairs = []
    for z in range(8):
        panel, i = divmod(z, 4)
        target = 4 * (1 - panel) + SERVES[m][i]
        for y in range(4):
            pair = (z * 4 + y, target * 4 + y)
            pairs.append(pair[::-1] if backwards else pair)
    return pairs


def neighbours(r):
    pairs = []
    for z in range(8):
        for y in range(4):
            target = z // 2 * 2 + (z + r // 4) % 2
            pairs.append((z * 4 + y, target * 4 + (y + r) % 4))
    return pairs


def shards(
    field,
    velocity,
    send_cells,
    block_size,
    donor_slot,
    intersection_weight,
    block_inverse,
    lower_coupling,
    upper_coupling,
):
    field = field.reshape(ROWS, CELLS)
    velocity = velocity.reshape(3 * DEPTH, CELLS)
    place = jnp.stack([lax.axis_index("ang"), lax.axis_index("rad")]).astype(jnp.int32)

    meta = jnp.concatenate([donor_slot.astype(f32), intersection_weight], axis=0)
    metas = [lax.ppermute(meta, "ang", crossing(m, True)) for m in range(2)]

    spread, rounded = pl.pallas_call(
        spread_kernel,
        grid=(PARTS,),
        in_specs=[
            SMEM,
            pl.BlockSpec((PART_ROWS, CELLS), lambda i: (i, 0)),
            whole((3 * DEPTH, CELLS)),
            whole((BLOCKS, DEPTH, DEPTH)),
        ],
        out_specs=[
            pl.BlockSpec((PART_ROWS, INNER), lambda i: (i, 0)),
            pl.BlockSpec((PART_ROWS, INNER), lambda i: (i, 0)),
        ],
        out_shape=[
            jax.ShapeDtypeStruct((ROWS, INNER), f32),
            jax.ShapeDtypeStruct((ROWS, INNER), bf16),
        ],
        scratch_shapes=[pltpu.VMEM((PART_ROWS, PART_ROWS), bf16)] * 2,
        compiler_params=params(14),
        name="spread",
    )(place, field, velocity, block_inverse)

    *lists, edges = pl.pallas_call(
        list_kernel,
        in_specs=[SMEM, SMEM] + [pl.BlockSpec(memory_space=pltpu.VMEM)] * 2,
        out_specs=[pl.BlockSpec(memory_space=pltpu.VMEM)] * (GROUP + 1),
        out_shape=[jax.ShapeDtypeStruct((ROWS, 2 * CAP), bf16)] * GROUP
        + [jax.ShapeDtypeStruct((BLOCKS, EDGE, 256), bf16)],
        compiler_params=params(14),
        name="lists",
    )(place, block_size, send_cells, rounded)

    donors = lists[:1] + [lax.ppermute(lists[r], "ang", neighbours(r)) for r in range(1, GROUP)]

    weights = pl.pallas_call(
        weight_kernel,
        in_specs=[SMEM, pl.BlockSpec(memory_space=pltpu.VMEM), pl.BlockSpec(memory_space=pltpu.VMEM)],
        out_specs=pl.BlockSpec(memory_space=pltpu.VMEM),
        out_shape=jax.ShapeDtypeStruct((2, GROUP * CAP, 2 * RIM), bf16),
        compiler_params=params(8),
        name="weights",
    )(place, *metas)

    needed, spikes = pl.pallas_call(
        setup_kernel,
        in_specs=[SMEM, SMEM, SMEM, SMEM, pl.BlockSpec(memory_space=pltpu.VMEM)],
        out_specs=[pl.BlockSpec(memory_space=pltpu.VMEM)] * 2,
        out_shape=[
            jax.ShapeDtypeStruct((2 * BLOCKS, 128), f32),
            jax.ShapeDtypeStruct((ROWS, 128), bf16),
        ],
        compiler_params=params(4),
        name="setup",
    )(place, lower_coupling, upper_coupling, block_inverse, block_inverse)

    exchanged = lax.all_to_all(edges, "rad", 0, 0)
    coupled = pl.pallas_call(
        solve_kernel,
        in_specs=[SMEM, pl.BlockSpec(memory_space=pltpu.VMEM)],
        out_specs=pl.BlockSpec(memory_space=pltpu.VMEM),
        out_shape=jax.ShapeDtypeStruct((BLOCKS, EDGE, 256), bf16),
        compiler_params=params(4),
        name="solve",
    )(needed, exchanged)
    coupled = lax.all_to_all(coupled, "rad", 0, 0)

    result = pl.pallas_call(
        finish_kernel,
        grid=(INNER // 256,),
        in_specs=[
            pl.BlockSpec((ROWS, 256), lambda i: (0, i)),
            whole((ROWS, 128)),
            pl.BlockSpec((1, EDGE, 256), lambda i: (i, 0, 0)),
        ],
        out_specs=pl.BlockSpec((ROWS, 256), lambda i: (0, i)),
        out_shape=jax.ShapeDtypeStruct((ROWS, CELLS), bf16),
        compiler_params=params(6),
        name="finish",
    )(spread, spikes, coupled)

    outs = pl.pallas_call(
        partial_kernel,
        in_specs=[pl.BlockSpec(memory_space=pltpu.VMEM)] * (GROUP + 1),
        out_specs=[pl.BlockSpec(memory_space=pltpu.VMEM)] * 4,
        out_shape=[jax.ShapeDtypeStruct((EDGE + EARLY, RIM), bf16)] * 2
        + [jax.ShapeDtypeStruct((ROWS - EARLY, RIM), bf16)] * 2,
        compiler_params=params(14),
        name="partial",
    )(weights, *donors)

    early = [lax.ppermute(outs[m], "ang", crossing(m, False)) for m in range(2)]
    late = [lax.ppermute(outs[2 + m], "ang", crossing(m, False)) for m in range(2)]

    ghost_edges = pl.pallas_call(
        join_kernel,
        in_specs=[pl.BlockSpec(memory_space=pltpu.VMEM)] * 2,
        out_specs=pl.BlockSpec(memory_space=pltpu.VMEM),
        out_shape=jax.ShapeDtypeStruct((EDGE, RIM), bf16),
        compiler_params=params(2),
        name="join",
    )(*early)
    all_edges = [ghost_edges] + [
        lax.ppermute(ghost_edges, "rad", [(k, (k + shift) % BLOCKS) for k in range(BLOCKS)])
        for shift in range(1, BLOCKS)
    ]

    result = pl.pallas_call(
        ghost_kernel,
        grid=(1,),
        in_specs=[SMEM, SMEM, pl.BlockSpec(memory_space=pl.ANY)]
        + [whole((EDGE + EARLY, RIM))] * 2
        + [whole((ROWS - EARLY, RIM))] * 2
        + [whole((EDGE, RIM))] * BLOCKS
        + [whole((ROWS, 128))],
        out_specs=pl.BlockSpec((ROWS, RIM), lambda i: (0, INNER // RIM)),
        out_shape=jax.ShapeDtypeStruct((ROWS, CELLS), bf16),
        input_output_aliases={2: 0},
        compiler_params=params(8),
        name="ghosts",
    )(place, needed, result, *early, *late, *all_edges, spikes)
    return result.reshape(CHANNELS, DEPTH, CELLS)


def solution(mesh):
    in_specs = (
        P(None, "rad", "ang"),
        P(None, "rad", "ang"),
        P("ang", None, None),
        P("ang", None),
        P(None, "ang"),
        P(None, "ang"),
        P(),
        P(),
        P(),
    )
    out_specs = P(None, "rad", "ang")
    return jax.shard_map(shards, mesh=mesh, in_specs=in_specs, out_specs=out_specs, check_vma=False)
```

```python
import jax
import jax.numpy as jnp
from jax import lax
from jax.experimental import pallas as pl
from jax.experimental.pallas import tpu as pltpu
from jax.sharding import PartitionSpec as P

f32 = jnp.float32
bf16 = jnp.bfloat16
highest = lax.Precision.HIGHEST
induction = 0.5

CHANNELS = 27
DEPTH = 16
ROWS = CHANNELS * DEPTH
CELLS = 2048
RIM = 256
INNER = CELLS - RIM
CAP = 128
TILES = 32
BLOCKS = 8
PARTS = 3
PART_ROWS = ROWS // PARTS
EDGE = 64
GROUP = 8

SERVES = ((3, 1, 2, 0), (2, 0, 3, 1))


def params(mebibytes):
    return pltpu.CompilerParams(vmem_limit_bytes=mebibytes * 1024 * 1024)


def iota(shape, axis):
    return lax.broadcasted_iota(jnp.int32, shape, axis)


def split(value):
    high = value.astype(bf16)
    return high, (value - high.astype(f32)).astype(bf16)


def dot(left, right):
    return jnp.dot(left, right, preferred_element_type=f32)


def edge_select(rows, channels, first):
    row, column = iota((EDGE, rows), 0), iota((EDGE, rows), 1)
    channel = row % 32 - first
    wanted = channel * DEPTH + (row // 32) * (DEPTH - 1)
    return ((channel >= 0) & (channel < channels) & (column == wanted)).astype(f32).astype(bf16)


def head_kernel(place, block_size, cells_hbm, field_hbm, velocity_hbm, inverse_hbm, *refs):
    spread_hbm, lists_hbm, chunks = refs[0], refs[1], refs[2 : 2 + BLOCKS]
    cells, field, velocity, own, spread, rounded, lists, edges, done, sent = refs[2 + BLOCKS :]
    copies = [
        pltpu.make_async_copy(inverse_hbm.at[place[1]], own, done.at[0]),
        pltpu.make_async_copy(velocity_hbm, velocity, done.at[1]),
    ]
    for part in range(PARTS):
        rows = pl.ds(part * PART_ROWS, PART_ROWS)
        copies.append(pltpu.make_async_copy(field_hbm.at[rows], field.at[rows], done.at[2 + part]))
    copies.append(pltpu.make_async_copy(cells_hbm, cells, done.at[2 + PARTS]))
    for copy in copies:
        copy.start()
    sends = []

    size = PART_ROWS
    rows = (iota((size, DEPTH), 0) % DEPTH == iota((size, DEPTH), 1)).astype(f32)
    columns = (iota((DEPTH, size), 1) % DEPTH == iota((DEPTH, size), 0)).astype(f32)
    same = iota((size, size), 0) // DEPTH == iota((size, size), 1) // DEPTH
    copies[0].wait()
    tiled = jnp.dot(jnp.dot(rows, own[...], precision=highest), columns, precision=highest)
    high_mat, low_mat = split(jnp.where(same, tiled, 0.0))

    copies[1].wait()
    flow = [velocity[DEPTH * i : DEPTH * (i + 1), :INNER].astype(f32) for i in range(3)]
    for part in range(PARTS):
        copies[2 + part].wait()
        sources = []
        for m in range(PART_ROWS // (3 * DEPTH)):
            first = part * PART_ROWS + 3 * m * DEPTH
            f = [
                field[first + DEPTH * i : first + DEPTH * (i + 1), :INNER].astype(f32)
                for i in range(3)
            ]
            for i in range(3):
                j, k = (i + 1) % 3, (i + 2) % 3
                sources.append(f[i] + induction * (flow[j] * f[k] - flow[k] * f[j]))
        source_high, source_low = split(jnp.concatenate(sources, axis=0))
        result = dot(high_mat, source_high) + dot(high_mat, source_low)
        result = result + dot(low_mat, source_high)
        here = slice(part * PART_ROWS, (part + 1) * PART_ROWS)
        spread[here, :] = result
        rounded[here, :] = result.astype(bf16)
        rows = pl.ds(part * PART_ROWS, PART_ROWS)
        sends.append(pltpu.make_async_copy(spread.at[rows], spread_hbm.at[rows], sent.at[part]))
        sends[-1].start()
    edges[:, :INNER] = dot(edge_select(ROWS, CHANNELS, 0), rounded[...]).astype(bf16)
    edges[:, INNER:] = jnp.zeros((EDGE, RIM), bf16)
    for shift in range(BLOCKS):
        first = pl.multiple_of((place[1] + shift) % BLOCKS * 256, 256)
        chunks[shift][...] = edges[:, pl.ds(first, 256)]
    copies[2 + PARTS].wait()

    row = place[0] // 4
    panel, half = row // 4, (row // 2) % 2
    for r in range(GROUP):
        member, y = r // 4, r % 4
        served = (3 - 2 * member - half, 2 - 2 * member + half)
        wanted = []
        for m in range(2):
            tile = (4 * (1 - panel) + served[m]) * 4 + y
            listed = cells[0, pl.ds(tile, 1), :]
            wanted.append(jnp.where(iota((1, CAP), 1) < block_size[0, tile], listed, -1))
        wanted = jnp.concatenate(wanted, axis=1)
        total = jnp.zeros((ROWS, 2 * CAP), f32)
        for first in range(0, INNER, 256):
            hot = (iota((256, 2 * CAP), 0) + first == wanted).astype(f32).astype(bf16)
            total = total + dot(rounded[:, first : first + 256], hot)
        lists[r] = total.astype(bf16)
        sends.append(pltpu.make_async_copy(lists.at[r], lists_hbm.at[r], sent.at[PARTS + r]))
        sends[-1].start()
    for copy in sends:
        copy.wait()


def weight_kernel(place, first, second, weights):
    base = place[0] // GROUP * GROUP
    for m, meta in enumerate((first, second)):
        slots = meta[0:4, :].astype(jnp.int32)
        for r in range(GROUP):
            position = iota((CAP, RIM), 0) + (base + r) * CAP
            value = jnp.zeros((CAP, RIM), f32)
            for d in range(4):
                value = value + jnp.where(slots[d : d + 1, :] == position, meta[4 + d : 5 + d, :], 0.0)
            high, low = split(value)
            weights[m, r * CAP : (r + 1) * CAP, :RIM] = high
            weights[m, r * CAP : (r + 1) * CAP, RIM:] = low


def setup_kernel(place, lower, upper, corner, block_inverse, needed, spikes):
    size = 2 * BLOCKS
    shape = (size, 128)
    row, lane = iota(shape, 0), iota(shape, 1)
    work = ((row == lane) | (row + size == lane)).astype(f32)
    for k in range(BLOCKS):
        for b in range(2):
            i = b * (DEPTH - 1)
            here = row == 2 * k + b
            if k < BLOCKS - 1:
                value = corner[k, i, DEPTH - 1] * upper[k]
                work = jnp.where(here & (lane == 2 * k + 2), value, work)
            if k > 0:
                value = corner[k, i, 0] * lower[k - 1]
                work = jnp.where(here & (lane == 2 * k - 1), value, work)
    for p in range(size):
        column = jnp.sum(jnp.where(lane == p, work, 0.0), axis=1, keepdims=True)
        chosen = work[p : p + 1, :] / column[p : p + 1, :]
        work = jnp.where(row == p, chosen, work - column * chosen)
    up = jnp.concatenate([work[2:, :], jnp.zeros((2, 128), f32)], axis=0)
    down = jnp.concatenate([jnp.zeros((2, 128), f32), work[:-2, :]], axis=0)
    needed[...] = jnp.where(row % 2 == 0, up, down)

    k = place[1]
    ahead = jnp.where(k < BLOCKS - 1, upper[jnp.minimum(k, BLOCKS - 2)], 0.0)
    behind = jnp.where(k > 0, lower[jnp.maximum(k - 1, 0)], 0.0)
    rows = (iota((ROWS, DEPTH), 0) % DEPTH == iota((ROWS, DEPTH), 1)).astype(f32)
    tiled = jnp.dot(rows, block_inverse[k], precision=highest)
    right, left = tiled[:, DEPTH - 1 :] * ahead, tiled[:, :1] * behind
    channel, lane = iota((ROWS, 128), 0) // DEPTH, iota((ROWS, 128), 1)
    full = jnp.where(lane % 64 == channel, right, 0.0)
    full = full + jnp.where(lane % 64 == channel + 32, left, 0.0)
    high, low = split(full)
    spikes[...] = jnp.where(lane < 64, high.astype(f32), low.astype(f32)).astype(bf16)


def partial_kernel(weights, lists, coupled, *outs):
    del coupled
    for m in range(2):
        values = [lists[r, :, m * CAP : (m + 1) * CAP] for r in range(GROUP)]
        both = dot(jnp.concatenate(values, axis=1), weights[m])
        result = (both[:, :RIM] + both[:, RIM:]).astype(bf16)
        outs[m][...] = dot(edge_select(ROWS, CHANNELS, 0), result).astype(bf16)
        outs[2 + m][...] = result


def solve_kernel(place, needed, *refs):
    chunks, coupled = refs[:BLOCKS], refs[BLOCKS]
    values = [chunks[shift][...].astype(f32) for shift in range(BLOCKS)]
    for k in range(BLOCKS):
        for p in range(2):
            total = jnp.zeros((32, 256), f32)
            for shift in range(BLOCKS):
                block = (place[1] + BLOCKS - shift) % BLOCKS
                for b in range(2):
                    factor = needed[2 * k + p, 2 * BLOCKS + 2 * block + b]
                    total = total + factor * values[shift][32 * b : 32 * b + 32, :]
            coupled[k, 32 * p : 32 * p + 32, :] = total.astype(bf16)


def join_kernel(first, second, coupled, moved, edges):
    del moved
    both = (first[...].astype(f32) + second[...].astype(f32)).astype(bf16)
    for k in range(BLOCKS):
        edges[k, :EDGE, :] = coupled[k]
        edges[k, EDGE:, :] = both


def finish_kernel(place, needed, spread, first, second, coupled, spikes, result):
    step = pl.program_id(0)

    @pl.when(step < INNER // 256)
    def _():
        mine = coupled[step, :EDGE, :]
        correction = dot(spikes[...], jnp.concatenate([mine, mine], axis=0))
        result[...] = (spread[...] - correction).astype(bf16)

    @pl.when(step == INNER // 256)
    def _():
        own = place[1]
        halves = []
        for p in range(2):
            total = jnp.zeros((32, RIM), f32)
            for k in range(BLOCKS):
                for b in range(2):
                    factor = needed[2 * own + p, 2 * BLOCKS + 2 * k + b]
                    edge = coupled[k, EDGE + 32 * b : EDGE + 32 * b + 32, :]
                    total = total + factor * edge.astype(f32)
            halves.append(total)
        mine = jnp.concatenate(halves, axis=0).astype(bf16)
        correction = dot(spikes[...], jnp.concatenate([mine, mine], axis=0))
        ghost = first[...].astype(f32) + second[...].astype(f32)
        result[...] = (ghost - correction).astype(bf16)


SMEM = pl.BlockSpec(memory_space=pltpu.SMEM)
VMEM = pl.BlockSpec(memory_space=pltpu.VMEM)
ANY = pl.BlockSpec(memory_space=pl.ANY)


def whole(shape):
    return pl.BlockSpec(shape, lambda i: (0,) * len(shape))


def crossing(m, backwards):
    pairs = []
    for z in range(8):
        panel, i = divmod(z, 4)
        target = 4 * (1 - panel) + SERVES[m][i]
        for y in range(4):
            pair = (z * 4 + y, target * 4 + y)
            pairs.append(pair[::-1] if backwards else pair)
    return pairs


def shards(
    field,
    velocity,
    send_cells,
    block_size,
    donor_slot,
    intersection_weight,
    block_inverse,
    lower_coupling,
    upper_coupling,
):
    field = field.reshape(ROWS, CELLS)
    velocity = velocity.reshape(3 * DEPTH, CELLS)
    place = jnp.stack([lax.axis_index("ang"), lax.axis_index("rad")]).astype(jnp.int32)

    meta = jnp.concatenate([donor_slot.astype(f32), intersection_weight], axis=0)
    metas = [lax.ppermute(meta, "ang", crossing(m, True)) for m in range(2)]

    groups = [list(range(g * GROUP, (g + 1) * GROUP)) for g in range(TILES // GROUP)]
    spread, lists, *chunks = pl.pallas_call(
        head_kernel,
        in_specs=[SMEM, SMEM] + [ANY] * 4,
        out_specs=[ANY] * 2 + [VMEM] * BLOCKS,
        out_shape=[
            jax.ShapeDtypeStruct((ROWS, INNER), f32),
            jax.ShapeDtypeStruct((GROUP, ROWS, 2 * CAP), bf16),
        ]
        + [jax.ShapeDtypeStruct((EDGE, 256), bf16)] * BLOCKS,
        scratch_shapes=[
            pltpu.VMEM((1, TILES, CAP), jnp.int32),
            pltpu.VMEM((ROWS, CELLS), bf16),
            pltpu.VMEM((3 * DEPTH, CELLS), bf16),
            pltpu.VMEM((DEPTH, DEPTH), f32),
            pltpu.VMEM((ROWS, INNER), f32),
            pltpu.VMEM((ROWS, INNER), bf16),
            pltpu.VMEM((GROUP, ROWS, 2 * CAP), bf16),
            pltpu.VMEM((EDGE, CELLS), bf16),
            pltpu.SemaphoreType.DMA((3 + PARTS,)),
            pltpu.SemaphoreType.DMA((PARTS + GROUP,)),
        ],
        compiler_params=params(60),
        name="head",
    )(place, block_size, send_cells, field, velocity, block_inverse)

    donors = lax.all_to_all(lists, "ang", 0, 0, axis_index_groups=groups)
    chunks = chunks[:1] + [
        lax.ppermute(chunks[shift], "rad", [(k, (k + shift) % BLOCKS) for k in range(BLOCKS)])
        for shift in range(1, BLOCKS)
    ]

    weights = pl.pallas_call(
        weight_kernel,
        in_specs=[SMEM, VMEM, VMEM],
        out_specs=VMEM,
        out_shape=jax.ShapeDtypeStruct((2, GROUP * CAP, 2 * RIM), bf16),
        compiler_params=params(8),
        name="weights",
    )(place, *metas)

    needed, spikes = pl.pallas_call(
        setup_kernel,
        in_specs=[SMEM, SMEM, SMEM, SMEM, VMEM],
        out_specs=[VMEM] * 2,
        out_shape=[
            jax.ShapeDtypeStruct((2 * BLOCKS, 128), f32),
            jax.ShapeDtypeStruct((ROWS, 128), bf16),
        ],
        compiler_params=params(4),
        name="setup",
    )(place, lower_coupling, upper_coupling, block_inverse, block_inverse)

    coupled = pl.pallas_call(
        solve_kernel,
        in_specs=[SMEM] * 2 + [VMEM] * BLOCKS,
        out_specs=VMEM,
        out_shape=jax.ShapeDtypeStruct((BLOCKS, EDGE, 256), bf16),
        compiler_params=params(4),
        name="solve",
    )(place, needed, *chunks)

    *first_edges, first, second = pl.pallas_call(
        partial_kernel,
        in_specs=[VMEM] * 2 + [ANY],
        out_specs=[VMEM] * 4,
        out_shape=[jax.ShapeDtypeStruct((EDGE, RIM), bf16)] * 2
        + [jax.ShapeDtypeStruct((ROWS, RIM), bf16)] * 2,
        compiler_params=params(14),
        name="partial",
    )(weights, donors, coupled)

    first_edges = [lax.ppermute(first_edges[m], "ang", crossing(m, False)) for m in range(2)]
    ghosts = [lax.ppermute(value, "ang", crossing(m, False)) for m, value in enumerate((first, second))]

    joined = pl.pallas_call(
        join_kernel,
        in_specs=[VMEM] * 3 + [ANY],
        out_specs=VMEM,
        out_shape=jax.ShapeDtypeStruct((BLOCKS, 2 * EDGE, RIM), bf16),
        compiler_params=params(4),
        name="join",
    )(*first_edges, coupled, ghosts[0])
    joined = lax.all_to_all(joined, "rad", 0, 0)

    result = pl.pallas_call(
        finish_kernel,
        grid=(CELLS // 256,),
        in_specs=[
            SMEM,
            SMEM,
            pl.BlockSpec((ROWS, 256), lambda i: (0, jnp.minimum(i, INNER // 256 - 1))),
            whole((ROWS, RIM)),
            whole((ROWS, RIM)),
            whole((BLOCKS, 2 * EDGE, 256)),
            whole((ROWS, 128)),
        ],
        out_specs=pl.BlockSpec((ROWS, 256), lambda i: (0, i)),
        out_shape=jax.ShapeDtypeStruct((ROWS, CELLS), bf16),
        compiler_params=params(61),
        name="finish",
    )(place, needed, spread, *ghosts, joined, spikes)
    return result.reshape(CHANNELS, DEPTH, CELLS)


def solution(mesh):
    in_specs = (
        P(None, "rad", "ang"),
        P(None, "rad", "ang"),
        P("ang", None, None),
        P("ang", None),
        P(None, "ang"),
        P(None, "ang"),
        P(),
        P(),
        P(),
    )
    out_specs = P(None, "rad", "ang")
    return jax.shard_map(shards, mesh=mesh, in_specs=in_specs, out_specs=out_specs, check_vma=False)
```

```python
import jax
import jax.numpy as jnp
from jax import lax
from jax.experimental import pallas as pl
from jax.experimental.pallas import tpu as pltpu
from jax.sharding import PartitionSpec as P

f32 = jnp.float32
bf16 = jnp.bfloat16
highest = lax.Precision.HIGHEST
induction = 0.5

CHANNELS = 27
DEPTH = 16
ROWS = CHANNELS * DEPTH
CELLS = 2048
RIM = 256
INNER = CELLS - RIM
CAP = 128
TILES = 32
BLOCKS = 8
PARTS = 3
PART_ROWS = ROWS // PARTS
EDGE = 64
GROUP = 8

SERVES = ((3, 1, 2, 0), (2, 0, 3, 1))


def params(mebibytes):
    return pltpu.CompilerParams(vmem_limit_bytes=mebibytes * 1024 * 1024)


def iota(shape, axis):
    return lax.broadcasted_iota(jnp.int32, shape, axis)


def split(value):
    high = value.astype(bf16)
    return high, (value - high.astype(f32)).astype(bf16)


def dot(left, right):
    return jnp.dot(left, right, preferred_element_type=f32)


def edge_select(rows, channels, first):
    row, column = iota((EDGE, rows), 0), iota((EDGE, rows), 1)
    channel = row % 32 - first
    wanted = channel * DEPTH + (row // 32) * (DEPTH - 1)
    return ((channel >= 0) & (channel < channels) & (column == wanted)).astype(f32).astype(bf16)


def head_kernel(place, block_size, cells_hbm, field_hbm, velocity_hbm, inverse_hbm, *refs):
    spread_hbm, lists_hbm, chunks = refs[0], refs[1], refs[2 : 2 + BLOCKS]
    cells, field, velocity, own, spread, rounded, lists, edges, done, sent = refs[2 + BLOCKS :]
    copies = [
        pltpu.make_async_copy(inverse_hbm.at[place[1]], own, done.at[0]),
        pltpu.make_async_copy(velocity_hbm, velocity, done.at[1]),
    ]
    for part in range(PARTS):
        rows = pl.ds(part * PART_ROWS, PART_ROWS)
        copies.append(pltpu.make_async_copy(field_hbm.at[rows], field.at[rows], done.at[2 + part]))
    copies.append(pltpu.make_async_copy(cells_hbm, cells, done.at[2 + PARTS]))
    for copy in copies:
        copy.start()
    sends = []

    size = PART_ROWS
    rows = (iota((size, DEPTH), 0) % DEPTH == iota((size, DEPTH), 1)).astype(f32)
    columns = (iota((DEPTH, size), 1) % DEPTH == iota((DEPTH, size), 0)).astype(f32)
    same = iota((size, size), 0) // DEPTH == iota((size, size), 1) // DEPTH
    copies[0].wait()
    tiled = jnp.dot(jnp.dot(rows, own[...], precision=highest), columns, precision=highest)
    high_mat, low_mat = split(jnp.where(same, tiled, 0.0))

    copies[1].wait()
    flow = [velocity[DEPTH * i : DEPTH * (i + 1), :INNER].astype(f32) for i in range(3)]
    for part in range(PARTS):
        copies[2 + part].wait()
        sources = []
        for m in range(PART_ROWS // (3 * DEPTH)):
            first = part * PART_ROWS + 3 * m * DEPTH
            f = [
                field[first + DEPTH * i : first + DEPTH * (i + 1), :INNER].astype(f32)
                for i in range(3)
            ]
            for i in range(3):
                j, k = (i + 1) % 3, (i + 2) % 3
                sources.append(f[i] + induction * (flow[j] * f[k] - flow[k] * f[j]))
        source_high, source_low = split(jnp.concatenate(sources, axis=0))
        result = dot(high_mat, source_high) + dot(high_mat, source_low)
        result = result + dot(low_mat, source_high)
        here = slice(part * PART_ROWS, (part + 1) * PART_ROWS)
        spread[here, :] = result
        rounded[here, :] = result.astype(bf16)
        rows = pl.ds(part * PART_ROWS, PART_ROWS)
        target = spread_hbm.at[rows, pl.ds(0, INNER)]
        sends.append(pltpu.make_async_copy(spread.at[rows], target, sent.at[part]))
        sends[-1].start()
    edges[:, :INNER] = dot(edge_select(ROWS, CHANNELS, 0), rounded[...]).astype(bf16)
    edges[:, INNER:] = jnp.zeros((EDGE, RIM), bf16)
    for shift in range(BLOCKS):
        first = pl.multiple_of((place[1] + shift) % BLOCKS * 256, 256)
        chunks[shift][...] = edges[:, pl.ds(first, 256)]
    copies[2 + PARTS].wait()

    row = place[0] // 4
    panel, half = row // 4, (row // 2) % 2
    for r in range(GROUP):
        member, y = r // 4, r % 4
        served = (3 - 2 * member - half, 2 - 2 * member + half)
        wanted = []
        for m in range(2):
            tile = (4 * (1 - panel) + served[m]) * 4 + y
            listed = cells[0, pl.ds(tile, 1), :]
            wanted.append(jnp.where(iota((1, CAP), 1) < block_size[0, tile], listed, -1))
        wanted = jnp.concatenate(wanted, axis=1)
        total = jnp.zeros((ROWS, 2 * CAP), f32)
        for first in range(0, INNER, 256):
            hot = (iota((256, 2 * CAP), 0) + first == wanted).astype(f32).astype(bf16)
            total = total + dot(rounded[:, first : first + 256], hot)
        lists[r] = total.astype(bf16)
        sends.append(pltpu.make_async_copy(lists.at[r], lists_hbm.at[r], sent.at[PARTS + r]))
        sends[-1].start()
    for copy in sends:
        copy.wait()


def setup_kernel(
    place, lower, upper, corner, block_inverse, slots, factors, needed, spikes, meta
):
    meta[:4, :] = slots[...].astype(f32)
    meta[4:, :] = factors[...]
    size = 2 * BLOCKS
    shape = (size, 128)
    row, lane = iota(shape, 0), iota(shape, 1)
    work = ((row == lane) | (row + size == lane)).astype(f32)
    for k in range(BLOCKS):
        for b in range(2):
            i = b * (DEPTH - 1)
            here = row == 2 * k + b
            if k < BLOCKS - 1:
                value = corner[k, i, DEPTH - 1] * upper[k]
                work = jnp.where(here & (lane == 2 * k + 2), value, work)
            if k > 0:
                value = corner[k, i, 0] * lower[k - 1]
                work = jnp.where(here & (lane == 2 * k - 1), value, work)
    for p in range(size):
        column = jnp.sum(jnp.where(lane == p, work, 0.0), axis=1, keepdims=True)
        chosen = work[p : p + 1, :] / column[p : p + 1, :]
        work = jnp.where(row == p, chosen, work - column * chosen)
    up = jnp.concatenate([work[2:, :], jnp.zeros((2, 128), f32)], axis=0)
    down = jnp.concatenate([jnp.zeros((2, 128), f32), work[:-2, :]], axis=0)
    needed[...] = jnp.where(row % 2 == 0, up, down)

    k = place[1]
    ahead = jnp.where(k < BLOCKS - 1, upper[jnp.minimum(k, BLOCKS - 2)], 0.0)
    behind = jnp.where(k > 0, lower[jnp.maximum(k - 1, 0)], 0.0)
    rows = (iota((ROWS, DEPTH), 0) % DEPTH == iota((ROWS, DEPTH), 1)).astype(f32)
    tiled = jnp.dot(rows, block_inverse[k], precision=highest)
    right, left = tiled[:, DEPTH - 1 :] * ahead, tiled[:, :1] * behind
    channel, lane = iota((ROWS, 128), 0) // DEPTH, iota((ROWS, 128), 1)
    full = jnp.where(lane % 64 == channel, right, 0.0)
    full = full + jnp.where(lane % 64 == channel + 32, left, 0.0)
    high, low = split(full)
    spikes[...] = jnp.where(lane < 64, high.astype(f32), low.astype(f32)).astype(bf16)


def partial_kernel(place, first_meta, second_meta, lists, coupled, first, second, shared):
    base = place[0] // GROUP * GROUP
    shared[:, :EDGE, :] = coupled[...]
    for m, (meta, partial) in enumerate(((first_meta, first), (second_meta, second))):
        slots = meta[:4, :].astype(jnp.int32) - base * CAP
        total = jnp.zeros((ROWS, RIM), f32)
        for r in range(0, GROUP, 2):
            position = iota((2 * CAP, RIM), 0) + r * CAP
            weights = jnp.zeros((2 * CAP, RIM), f32)
            for d in range(4):
                hit = slots[d : d + 1, :] == position
                weights = weights + jnp.where(hit, meta[4 + d : 5 + d, :], 0.0)
            columns = slice(m * CAP, (m + 1) * CAP)
            values = jnp.concatenate([lists[r, :, columns], lists[r + 1, :, columns]], axis=1)
            total = total + dot(values, weights.astype(bf16))
        result = total.astype(bf16)
        partial[...] = result
        edges = dot(edge_select(ROWS, CHANNELS, 0), result).astype(bf16)
        for k in range(BLOCKS):
            shared[k, EDGE * (m + 1) : EDGE * (m + 2), :] = edges


def solve_kernel(place, needed, meta, *refs):
    chunks, coupled, passed = refs[:BLOCKS], refs[BLOCKS], refs[BLOCKS + 1]
    passed[...] = meta[...]
    values = [chunks[shift][...].astype(f32) for shift in range(BLOCKS)]
    for k in range(BLOCKS):
        for p in range(2):
            total = jnp.zeros((32, 256), f32)
            for shift in range(BLOCKS):
                block = (place[1] + BLOCKS - shift) % BLOCKS
                for b in range(2):
                    factor = needed[2 * k + p, 2 * BLOCKS + 2 * block + b]
                    total = total + factor * values[shift][32 * b : 32 * b + 32, :]
            coupled[k, 32 * p : 32 * p + 32, :] = total.astype(bf16)


def own_kernel(place, needed, shared, *outs):
    own = place[1]
    for m in range(2):
        for p in range(2):
            total = jnp.zeros((32, RIM), f32)
            for k in range(BLOCKS):
                for b in range(2):
                    factor = needed[2 * own + p, 2 * BLOCKS + 2 * k + b]
                    row = EDGE * (m + 1) + 32 * b
                    total = total + factor * shared[k, row : row + 32, :].astype(f32)
            outs[m][32 * p : 32 * p + 32, :] = total.astype(bf16)


def finish_kernel(spread, shared, spikes, result):
    for j in range(2):
        here = slice(256 * j, 256 * (j + 1))
        coupled = shared[j, :EDGE, :]
        correction = dot(spikes[...], jnp.concatenate([coupled, coupled], axis=0))
        result[:, here] = (spread[:, here] - correction).astype(bf16)


def ghost_kernel(whole, first, second, first_coupled, second_coupled, spikes, result):
    del whole
    high, low = split(first_coupled[...].astype(f32) + second_coupled[...].astype(f32))
    correction = dot(spikes[...], jnp.concatenate([high, high], axis=0))
    correction = correction + dot(spikes[:, :EDGE], low)
    ghost = first[...].astype(f32) + second[...].astype(f32)
    result[...] = (ghost - correction).astype(bf16)


SMEM = pl.BlockSpec(memory_space=pltpu.SMEM)
VMEM = pl.BlockSpec(memory_space=pltpu.VMEM)
ANY = pl.BlockSpec(memory_space=pl.ANY)


def whole(shape):
    return pl.BlockSpec(shape, lambda i: (0,) * len(shape))


def crossing(m, backwards):
    pairs = []
    for z in range(8):
        panel, i = divmod(z, 4)
        target = 4 * (1 - panel) + SERVES[m][i]
        for y in range(4):
            pair = (z * 4 + y, target * 4 + y)
            pairs.append(pair[::-1] if backwards else pair)
    return pairs


def shards(
    field,
    velocity,
    send_cells,
    block_size,
    donor_slot,
    intersection_weight,
    block_inverse,
    lower_coupling,
    upper_coupling,
):
    field = field.reshape(ROWS, CELLS)
    velocity = velocity.reshape(3 * DEPTH, CELLS)
    place = jnp.stack([lax.axis_index("ang"), lax.axis_index("rad")]).astype(jnp.int32)

    groups = [list(range(g * GROUP, (g + 1) * GROUP)) for g in range(TILES // GROUP)]
    spread, lists, *chunks = pl.pallas_call(
        head_kernel,
        in_specs=[SMEM, SMEM] + [ANY] * 4,
        out_specs=[ANY] * 2 + [VMEM] * BLOCKS,
        out_shape=[
            jax.ShapeDtypeStruct((ROWS, CELLS), f32),
            jax.ShapeDtypeStruct((GROUP, ROWS, 2 * CAP), bf16),
        ]
        + [jax.ShapeDtypeStruct((EDGE, 256), bf16)] * BLOCKS,
        scratch_shapes=[
            pltpu.VMEM((1, TILES, CAP), jnp.int32),
            pltpu.VMEM((ROWS, CELLS), bf16),
            pltpu.VMEM((3 * DEPTH, CELLS), bf16),
            pltpu.VMEM((DEPTH, DEPTH), f32),
            pltpu.VMEM((ROWS, INNER), f32),
            pltpu.VMEM((ROWS, INNER), bf16),
            pltpu.VMEM((GROUP, ROWS, 2 * CAP), bf16),
            pltpu.VMEM((EDGE, CELLS), bf16),
            pltpu.SemaphoreType.DMA((3 + PARTS,)),
            pltpu.SemaphoreType.DMA((PARTS + GROUP,)),
        ],
        compiler_params=params(60),
        name="head",
    )(place, block_size, send_cells, field, velocity, block_inverse)

    donors = lax.all_to_all(lists, "ang", 0, 0, axis_index_groups=groups)
    chunks = chunks[:1] + [
        lax.ppermute(chunks[shift], "rad", [(k, (k + shift) % BLOCKS) for k in range(BLOCKS)])
        for shift in range(1, BLOCKS)
    ]

    needed, spikes, meta = pl.pallas_call(
        setup_kernel,
        in_specs=[SMEM, SMEM, SMEM, SMEM] + [VMEM] * 3,
        out_specs=[VMEM] * 3,
        out_shape=[
            jax.ShapeDtypeStruct((2 * BLOCKS, 128), f32),
            jax.ShapeDtypeStruct((ROWS, 128), bf16),
            jax.ShapeDtypeStruct((8, RIM), f32),
        ],
        compiler_params=params(4),
        name="setup",
    )(
        place,
        lower_coupling,
        upper_coupling,
        block_inverse,
        block_inverse,
        donor_slot,
        intersection_weight,
    )

    coupled, meta = pl.pallas_call(
        solve_kernel,
        in_specs=[SMEM] * 2 + [VMEM] * (BLOCKS + 1),
        out_specs=[VMEM] * 2,
        out_shape=[
            jax.ShapeDtypeStruct((BLOCKS, EDGE, 256), bf16),
            jax.ShapeDtypeStruct((8, RIM), f32),
        ],
        compiler_params=params(4),
        name="solve",
    )(place, needed, meta, *chunks)

    metas = [lax.ppermute(meta, "ang", crossing(m, True)) for m in range(2)]
    first, second, shared = pl.pallas_call(
        partial_kernel,
        in_specs=[SMEM] + [VMEM] * 4,
        out_specs=[VMEM] * 3,
        out_shape=[
            jax.ShapeDtypeStruct((ROWS, RIM), bf16),
            jax.ShapeDtypeStruct((ROWS, RIM), bf16),
            jax.ShapeDtypeStruct((BLOCKS, 3 * EDGE, 256), bf16),
        ],
        compiler_params=params(14),
        name="partial",
    )(place, *metas, donors, coupled)

    shared = lax.all_to_all(shared, "rad", 0, 0)
    ghosts = [lax.ppermute(value, "ang", crossing(m, False)) for m, value in enumerate((first, second))]

    own = pl.pallas_call(
        own_kernel,
        in_specs=[SMEM] * 2 + [VMEM],
        out_specs=[VMEM] * 2,
        out_shape=[jax.ShapeDtypeStruct((EDGE, RIM), bf16)] * 2,
        compiler_params=params(4),
        name="own",
    )(place, needed, shared)
    own = [lax.ppermute(value, "ang", crossing(m, False)) for m, value in enumerate(own)]

    result = pl.pallas_call(
        finish_kernel,
        grid=(CELLS // 512,),
        in_specs=[
            pl.BlockSpec((ROWS, 512), lambda i: (0, i)),
            pl.BlockSpec((2, 3 * EDGE, 256), lambda i: (i, 0, 0)),
            whole((ROWS, 128)),
        ],
        out_specs=pl.BlockSpec((ROWS, 512), lambda i: (0, i)),
        out_shape=jax.ShapeDtypeStruct((ROWS, CELLS), bf16),
        compiler_params=params(6),
        name="finish",
    )(spread, shared, spikes)

    result = pl.pallas_call(
        ghost_kernel,
        grid=(1,),
        in_specs=[ANY] + [whole((ROWS, RIM))] * 2 + [whole((EDGE, RIM))] * 2 + [whole((ROWS, 128))],
        out_specs=pl.BlockSpec((ROWS, RIM), lambda i: (0, INNER // RIM)),
        out_shape=jax.ShapeDtypeStruct((ROWS, CELLS), bf16),
        input_output_aliases={0: 0},
        compiler_params=params(6),
        name="ghosts",
    )(result, *ghosts, *own, spikes)
    return result.reshape(CHANNELS, DEPTH, CELLS)


def solution(mesh):
    in_specs = (
        P(None, "rad", "ang"),
        P(None, "rad", "ang"),
        P("ang", None, None),
        P("ang", None),
        P(None, "ang"),
        P(None, "ang"),
        P(),
        P(),
        P(),
    )
    out_specs = P(None, "rad", "ang")
    return jax.shard_map(shards, mesh=mesh, in_specs=in_specs, out_specs=out_specs, check_vma=False)
```

```python
import jax
import jax.numpy as jnp
from jax import lax
from jax.experimental import pallas as pl
from jax.experimental.pallas import tpu as pltpu
from jax.sharding import PartitionSpec as P

f32 = jnp.float32
bf16 = jnp.bfloat16
highest = lax.Precision.HIGHEST
induction = 0.5

CHANNELS = 27
DEPTH = 16
ROWS = CHANNELS * DEPTH
CELLS = 2048
RIM = 256
INNER = CELLS - RIM
CAP = 128
TILES = 32
BLOCKS = 8
PARTS = 3
PART_ROWS = ROWS // PARTS
EDGE = 64
GROUP = 8

SERVES = ((3, 1, 2, 0), (2, 0, 3, 1))


def params(mebibytes):
    return pltpu.CompilerParams(vmem_limit_bytes=mebibytes * 1024 * 1024)


def iota(shape, axis):
    return lax.broadcasted_iota(jnp.int32, shape, axis)


def split(value):
    high = value.astype(bf16)
    return high, (value - high.astype(f32)).astype(bf16)


def dot(left, right):
    return jnp.dot(left, right, preferred_element_type=f32)


def edge_select(rows, channels, first):
    row, column = iota((EDGE, rows), 0), iota((EDGE, rows), 1)
    channel = row % 32 - first
    wanted = channel * DEPTH + (row // 32) * (DEPTH - 1)
    return ((channel >= 0) & (channel < channels) & (column == wanted)).astype(f32).astype(bf16)


def head_kernel(block_size, cells_hbm, field_hbm, velocity_hbm, inverse_hbm, *refs):
    spread_hbm, lists_hbm, chunks = refs[0], refs[1], refs[2 : 2 + BLOCKS]
    cells, field, velocity, own, spread, rounded, lists, edges, done, sent = refs[2 + BLOCKS :]
    copies = [
        pltpu.make_async_copy(inverse_hbm.at[lax.axis_index("rad")], own, done.at[0]),
        pltpu.make_async_copy(velocity_hbm, velocity, done.at[1]),
    ]
    for part in range(PARTS):
        rows = pl.ds(part * PART_ROWS, PART_ROWS)
        copies.append(pltpu.make_async_copy(field_hbm.at[rows], field.at[rows], done.at[2 + part]))
    copies.append(pltpu.make_async_copy(cells_hbm, cells, done.at[2 + PARTS]))
    for copy in copies:
        copy.start()
    sends = []

    size = PART_ROWS
    rows = (iota((size, DEPTH), 0) % DEPTH == iota((size, DEPTH), 1)).astype(f32)
    columns = (iota((DEPTH, size), 1) % DEPTH == iota((DEPTH, size), 0)).astype(f32)
    same = iota((size, size), 0) // DEPTH == iota((size, size), 1) // DEPTH
    copies[0].wait()
    tiled = jnp.dot(jnp.dot(rows, own[...], precision=highest), columns, precision=highest)
    high_mat, low_mat = split(jnp.where(same, tiled, 0.0))
    matrix = jnp.concatenate([high_mat.astype(f32), high_mat.astype(f32), low_mat.astype(f32)], axis=1)
    matrix = matrix.astype(bf16)

    copies[1].wait()
    flow = [velocity[DEPTH * i : DEPTH * (i + 1), :INNER].astype(f32) for i in range(3)]
    for part in range(PARTS):
        copies[2 + part].wait()
        sources = []
        for m in range(PART_ROWS // (3 * DEPTH)):
            first = part * PART_ROWS + 3 * m * DEPTH
            f = [
                field[first + DEPTH * i : first + DEPTH * (i + 1), :INNER].astype(f32)
                for i in range(3)
            ]
            for i in range(3):
                j, k = (i + 1) % 3, (i + 2) % 3
                sources.append(f[i] + induction * (flow[j] * f[k] - flow[k] * f[j]))
        source_high, source_low = split(jnp.concatenate(sources, axis=0))
        result = dot(matrix, jnp.concatenate([source_high, source_low, source_high], axis=0))
        here = slice(part * PART_ROWS, (part + 1) * PART_ROWS)
        spread[here, :] = result
        rounded[here, :] = result.astype(bf16)
        rows = pl.ds(part * PART_ROWS, PART_ROWS)
        target = spread_hbm.at[rows, pl.ds(0, INNER)]
        sends.append(pltpu.make_async_copy(spread.at[rows], target, sent.at[part]))
        sends[-1].start()
    edges[:, :INNER] = dot(edge_select(ROWS, CHANNELS, 0), rounded[...]).astype(bf16)
    edges[:, INNER:] = jnp.zeros((EDGE, RIM), bf16)
    for shift in range(BLOCKS):
        first = pl.multiple_of((lax.axis_index("rad") + shift) % BLOCKS * 256, 256)
        chunks[shift][...] = edges[:, pl.ds(first, 256)]
    copies[2 + PARTS].wait()

    row = lax.axis_index("ang") // 4
    panel, half = row // 4, (row // 2) % 2
    for r in range(GROUP):
        member, y = r // 4, r % 4
        served = (3 - 2 * member - half, 2 - 2 * member + half)
        wanted = []
        for m in range(2):
            tile = (4 * (1 - panel) + served[m]) * 4 + y
            listed = cells[0, pl.ds(tile, 1), :]
            wanted.append(jnp.where(iota((1, CAP), 1) < block_size[0, tile], listed, -1))
        wanted = jnp.concatenate(wanted, axis=1)
        hot = (iota((INNER, 2 * CAP), 0) == wanted).astype(f32).astype(bf16)
        lists[r] = dot(rounded[...], hot).astype(bf16)
        sends.append(pltpu.make_async_copy(lists.at[r], lists_hbm.at[r], sent.at[PARTS + r]))
        sends[-1].start()
    for copy in sends:
        copy.wait()


def setup_kernel(
    lower, upper, corner, block_inverse, slots, factors, needed, spikes, meta
):
    meta[:4, :] = slots[...].astype(f32)
    meta[4:, :] = factors[...]
    size = 2 * BLOCKS
    shape = (size, 128)
    row, lane = iota(shape, 0), iota(shape, 1)
    work = ((row == lane) | (row + size == lane)).astype(f32)
    for k in range(BLOCKS):
        for b in range(2):
            i = b * (DEPTH - 1)
            here = row == 2 * k + b
            if k < BLOCKS - 1:
                value = corner[k, i, DEPTH - 1] * upper[k]
                work = jnp.where(here & (lane == 2 * k + 2), value, work)
            if k > 0:
                value = corner[k, i, 0] * lower[k - 1]
                work = jnp.where(here & (lane == 2 * k - 1), value, work)
    for p in range(size):
        column = jnp.sum(jnp.where(lane == p, work, 0.0), axis=1, keepdims=True)
        chosen = work[p : p + 1, :] / column[p : p + 1, :]
        work = jnp.where(row == p, chosen, work - column * chosen)
    up = jnp.concatenate([work[2:, :], jnp.zeros((2, 128), f32)], axis=0)
    down = jnp.concatenate([jnp.zeros((2, 128), f32), work[:-2, :]], axis=0)
    needed[...] = jnp.where(row % 2 == 0, up, down)

    k = lax.axis_index("rad")
    ahead = jnp.where(k < BLOCKS - 1, upper[jnp.minimum(k, BLOCKS - 2)], 0.0)
    behind = jnp.where(k > 0, lower[jnp.maximum(k - 1, 0)], 0.0)
    rows = (iota((ROWS, DEPTH), 0) % DEPTH == iota((ROWS, DEPTH), 1)).astype(f32)
    tiled = jnp.dot(rows, block_inverse[k], precision=highest)
    right, left = tiled[:, DEPTH - 1 :] * ahead, tiled[:, :1] * behind
    channel, lane = iota((ROWS, 128), 0) // DEPTH, iota((ROWS, 128), 1)
    full = jnp.where(lane % 64 == channel, right, 0.0)
    full = full + jnp.where(lane % 64 == channel + 32, left, 0.0)
    high, low = split(full)
    spikes[...] = jnp.where(lane < 64, high.astype(f32), low.astype(f32)).astype(bf16)


def partial_kernel(first_meta, second_meta, lists, coupled, first, second, shared):
    base = lax.axis_index("ang") // GROUP * GROUP
    shared[:, :EDGE, :] = coupled[...]
    for m, (meta, partial) in enumerate(((first_meta, first), (second_meta, second))):
        slots = meta[:4, :].astype(jnp.int32) - base * CAP
        position = iota((GROUP * CAP, RIM), 0)
        weights = jnp.zeros((GROUP * CAP, RIM), f32)
        for d in range(4):
            hit = slots[d : d + 1, :] == position
            weights = weights + jnp.where(hit, meta[4 + d : 5 + d, :], 0.0)
        values = [lists[r, :, m * CAP : (m + 1) * CAP] for r in range(GROUP)]
        result = dot(jnp.concatenate(values, axis=1), weights.astype(bf16)).astype(bf16)
        partial[...] = result
        edges = dot(edge_select(ROWS, CHANNELS, 0), result).astype(bf16)
        for k in range(BLOCKS):
            shared[k, EDGE * (m + 1) : EDGE * (m + 2), :] = edges


def solve_kernel(needed, meta, *refs):
    chunks, coupled, passed = refs[:BLOCKS], refs[BLOCKS], refs[BLOCKS + 1]
    passed[...] = meta[...]
    values = [chunks[shift][...].astype(f32) for shift in range(BLOCKS)]
    for k in range(BLOCKS):
        for p in range(2):
            total = jnp.zeros((32, 256), f32)
            for shift in range(BLOCKS):
                block = (lax.axis_index("rad") + BLOCKS - shift) % BLOCKS
                for b in range(2):
                    factor = needed[2 * k + p, 2 * BLOCKS + 2 * block + b]
                    total = total + factor * values[shift][32 * b : 32 * b + 32, :]
            coupled[k, 32 * p : 32 * p + 32, :] = total.astype(bf16)


def own_kernel(needed, shared, *outs):
    own = lax.axis_index("rad")
    for m in range(2):
        for p in range(2):
            total = jnp.zeros((32, RIM), f32)
            for k in range(BLOCKS):
                for b in range(2):
                    factor = needed[2 * own + p, 2 * BLOCKS + 2 * k + b]
                    row = EDGE * (m + 1) + 32 * b
                    total = total + factor * shared[k, row : row + 32, :].astype(f32)
            outs[m][32 * p : 32 * p + 32, :] = total.astype(bf16)


def finish_kernel(spread, shared, spikes, result):
    for j in range(2):
        here = slice(256 * j, 256 * (j + 1))
        coupled = shared[j, :EDGE, :]
        correction = dot(spikes[...], jnp.concatenate([coupled, coupled], axis=0))
        result[:, here] = (spread[:, here] - correction).astype(bf16)


def ghost_kernel(whole, first, second, first_coupled, second_coupled, spikes, result):
    del whole
    high, low = split(first_coupled[...].astype(f32) + second_coupled[...].astype(f32))
    correction = dot(spikes[...], jnp.concatenate([high, high], axis=0))
    correction = correction + dot(spikes[:, :EDGE], low)
    ghost = first[...].astype(f32) + second[...].astype(f32)
    result[...] = (ghost - correction).astype(bf16)


SMEM = pl.BlockSpec(memory_space=pltpu.SMEM)
VMEM = pl.BlockSpec(memory_space=pltpu.VMEM)
ANY = pl.BlockSpec(memory_space=pl.ANY)


def whole(shape):
    return pl.BlockSpec(shape, lambda i: (0,) * len(shape))


def crossing(m, backwards):
    pairs = []
    for z in range(8):
        panel, i = divmod(z, 4)
        target = 4 * (1 - panel) + SERVES[m][i]
        for y in range(4):
            pair = (z * 4 + y, target * 4 + y)
            pairs.append(pair[::-1] if backwards else pair)
    return pairs


def shards(
    field,
    velocity,
    send_cells,
    block_size,
    donor_slot,
    intersection_weight,
    block_inverse,
    lower_coupling,
    upper_coupling,
):
    field = field.reshape(ROWS, CELLS)
    velocity = velocity.reshape(3 * DEPTH, CELLS)

    groups = [list(range(g * GROUP, (g + 1) * GROUP)) for g in range(TILES // GROUP)]
    spread, lists, *chunks = pl.pallas_call(
        head_kernel,
        in_specs=[SMEM] + [ANY] * 4,
        out_specs=[ANY] * 2 + [VMEM] * BLOCKS,
        out_shape=[
            jax.ShapeDtypeStruct((ROWS, CELLS), f32),
            jax.ShapeDtypeStruct((GROUP, ROWS, 2 * CAP), bf16),
        ]
        + [jax.ShapeDtypeStruct((EDGE, 256), bf16)] * BLOCKS,
        scratch_shapes=[
            pltpu.VMEM((1, TILES, CAP), jnp.int32),
            pltpu.VMEM((ROWS, CELLS), bf16),
            pltpu.VMEM((3 * DEPTH, CELLS), bf16),
            pltpu.VMEM((DEPTH, DEPTH), f32),
            pltpu.VMEM((ROWS, INNER), f32),
            pltpu.VMEM((ROWS, INNER), bf16),
            pltpu.VMEM((GROUP, ROWS, 2 * CAP), bf16),
            pltpu.VMEM((EDGE, CELLS), bf16),
            pltpu.SemaphoreType.DMA((3 + PARTS,)),
            pltpu.SemaphoreType.DMA((PARTS + GROUP,)),
        ],
        compiler_params=params(60),
        name="head",
    )(block_size, send_cells, field, velocity, block_inverse)

    donors = lax.all_to_all(lists, "ang", 0, 0, axis_index_groups=groups)
    chunks = chunks[:1] + [
        lax.ppermute(chunks[shift], "rad", [(k, (k + shift) % BLOCKS) for k in range(BLOCKS)])
        for shift in range(1, BLOCKS)
    ]

    needed, spikes, meta = pl.pallas_call(
        setup_kernel,
        in_specs=[SMEM] * 3 + [VMEM] * 3,
        out_specs=[VMEM] * 3,
        out_shape=[
            jax.ShapeDtypeStruct((2 * BLOCKS, 128), f32),
            jax.ShapeDtypeStruct((ROWS, 128), bf16),
            jax.ShapeDtypeStruct((8, RIM), f32),
        ],
        compiler_params=params(4),
        name="setup",
    )(
        lower_coupling,
        upper_coupling,
        block_inverse,
        block_inverse,
        donor_slot,
        intersection_weight,
    )

    coupled, meta = pl.pallas_call(
        solve_kernel,
        in_specs=[SMEM] + [VMEM] * (BLOCKS + 1),
        out_specs=[VMEM] * 2,
        out_shape=[
            jax.ShapeDtypeStruct((BLOCKS, EDGE, 256), bf16),
            jax.ShapeDtypeStruct((8, RIM), f32),
        ],
        compiler_params=params(4),
        name="solve",
    )(needed, meta, *chunks)

    metas = [lax.ppermute(meta, "ang", crossing(m, True)) for m in range(2)]
    first, second, shared = pl.pallas_call(
        partial_kernel,
        in_specs=[VMEM] * 4,
        out_specs=[VMEM] * 3,
        out_shape=[
            jax.ShapeDtypeStruct((ROWS, RIM), bf16),
            jax.ShapeDtypeStruct((ROWS, RIM), bf16),
            jax.ShapeDtypeStruct((BLOCKS, 3 * EDGE, 256), bf16),
        ],
        compiler_params=params(14),
        name="partial",
    )(*metas, donors, coupled)

    shared = lax.all_to_all(shared, "rad", 0, 0)
    ghosts = [lax.ppermute(value, "ang", crossing(m, False)) for m, value in enumerate((first, second))]

    own = pl.pallas_call(
        own_kernel,
        in_specs=[SMEM, VMEM],
        out_specs=[VMEM] * 2,
        out_shape=[jax.ShapeDtypeStruct((EDGE, RIM), bf16)] * 2,
        compiler_params=params(4),
        name="own",
    )(needed, shared)
    own = [lax.ppermute(value, "ang", crossing(m, False)) for m, value in enumerate(own)]

    result = pl.pallas_call(
        finish_kernel,
        grid=(CELLS // 512,),
        in_specs=[
            pl.BlockSpec((ROWS, 512), lambda i: (0, i)),
            pl.BlockSpec((2, 3 * EDGE, 256), lambda i: (i, 0, 0)),
            whole((ROWS, 128)),
        ],
        out_specs=pl.BlockSpec((ROWS, 512), lambda i: (0, i)),
        out_shape=jax.ShapeDtypeStruct((ROWS, CELLS), bf16),
        compiler_params=params(6),
        name="finish",
    )(spread, shared, spikes)

    result = pl.pallas_call(
        ghost_kernel,
        grid=(1,),
        in_specs=[ANY] + [whole((ROWS, RIM))] * 2 + [whole((EDGE, RIM))] * 2 + [whole((ROWS, 128))],
        out_specs=pl.BlockSpec((ROWS, RIM), lambda i: (0, INNER // RIM)),
        out_shape=jax.ShapeDtypeStruct((ROWS, CELLS), bf16),
        input_output_aliases={0: 0},
        compiler_params=params(6),
        name="ghosts",
    )(result, *ghosts, *own, spikes)
    return result.reshape(CHANNELS, DEPTH, CELLS)


def solution(mesh):
    in_specs = (
        P(None, "rad", "ang"),
        P(None, "rad", "ang"),
        P("ang", None, None),
        P("ang", None),
        P(None, "ang"),
        P(None, "ang"),
        P(),
        P(),
        P(),
    )
    out_specs = P(None, "rad", "ang")
    return jax.shard_map(shards, mesh=mesh, in_specs=in_specs, out_specs=out_specs, check_vma=False)
```

```python
import jax
import jax.numpy as jnp
from jax import lax
from jax.experimental import pallas as pl
from jax.experimental.pallas import tpu as pltpu
from jax.sharding import PartitionSpec as P

f32 = jnp.float32
bf16 = jnp.bfloat16
highest = lax.Precision.HIGHEST
induction = 0.5

CHANNELS = 27
DEPTH = 16
ROWS = CHANNELS * DEPTH
CELLS = 2048
RIM = 256
INNER = CELLS - RIM
CAP = 128
TILES = 32
BLOCKS = 8
PARTS = 3
PART_ROWS = ROWS // PARTS
EDGE = 64
GROUP = 8

SERVES = ((3, 2, 1, 0), (1, 0, 3, 2))


def params(mebibytes):
    return pltpu.CompilerParams(vmem_limit_bytes=mebibytes * 1024 * 1024)


def iota(shape, axis):
    return lax.broadcasted_iota(jnp.int32, shape, axis)


def split(value):
    high = value.astype(bf16)
    return high, (value - high.astype(f32)).astype(bf16)


def dot(left, right):
    return jnp.dot(left, right, preferred_element_type=f32)


def edge_select(rows, channels, first):
    row, column = iota((EDGE, rows), 0), iota((EDGE, rows), 1)
    channel = row % 32 - first
    wanted = channel * DEPTH + (row // 32) * (DEPTH - 1)
    return ((channel >= 0) & (channel < channels) & (column == wanted)).astype(f32).astype(bf16)


def head_kernel(block_size, cells_hbm, field_hbm, velocity_hbm, inverse_hbm, *refs):
    spread_hbm, lists_hbm, chunks = refs[0], refs[1], refs[2 : 2 + BLOCKS]
    cells, field, velocity, own, spread, rounded, lists, edges, done, sent = refs[2 + BLOCKS :]
    copies = [
        pltpu.make_async_copy(inverse_hbm.at[lax.axis_index("rad")], own, done.at[0]),
        pltpu.make_async_copy(velocity_hbm, velocity, done.at[1]),
    ]
    for part in range(PARTS):
        rows = pl.ds(part * PART_ROWS, PART_ROWS)
        copies.append(pltpu.make_async_copy(field_hbm.at[rows], field.at[rows], done.at[2 + part]))
    copies.append(pltpu.make_async_copy(cells_hbm, cells, done.at[2 + PARTS]))
    for copy in copies:
        copy.start()
    sends = []

    size = PART_ROWS
    rows = (iota((size, DEPTH), 0) % DEPTH == iota((size, DEPTH), 1)).astype(f32)
    columns = (iota((DEPTH, size), 1) % DEPTH == iota((DEPTH, size), 0)).astype(f32)
    same = iota((size, size), 0) // DEPTH == iota((size, size), 1) // DEPTH
    copies[0].wait()
    tiled = jnp.dot(jnp.dot(rows, own[...], precision=highest), columns, precision=highest)
    high_mat, low_mat = split(jnp.where(same, tiled, 0.0))
    matrix = jnp.concatenate([high_mat.astype(f32), high_mat.astype(f32), low_mat.astype(f32)], axis=1)
    matrix = matrix.astype(bf16)

    copies[1].wait()
    flow = [velocity[DEPTH * i : DEPTH * (i + 1), :INNER].astype(f32) for i in range(3)]
    for part in range(PARTS):
        copies[2 + part].wait()
        sources = []
        for m in range(PART_ROWS // (3 * DEPTH)):
            first = part * PART_ROWS + 3 * m * DEPTH
            f = [
                field[first + DEPTH * i : first + DEPTH * (i + 1), :INNER].astype(f32)
                for i in range(3)
            ]
            for i in range(3):
                j, k = (i + 1) % 3, (i + 2) % 3
                sources.append(f[i] + induction * (flow[j] * f[k] - flow[k] * f[j]))
        source_high, source_low = split(jnp.concatenate(sources, axis=0))
        result = dot(matrix, jnp.concatenate([source_high, source_low, source_high], axis=0))
        here = slice(part * PART_ROWS, (part + 1) * PART_ROWS)
        spread[here, :] = result
        rounded[here, :] = result.astype(bf16)
        rows = pl.ds(part * PART_ROWS, PART_ROWS)
        target = spread_hbm.at[rows, pl.ds(0, INNER)]
        sends.append(pltpu.make_async_copy(spread.at[rows], target, sent.at[part]))
        sends[-1].start()
    edges[:, :INNER] = dot(edge_select(ROWS, CHANNELS, 0), rounded[...]).astype(bf16)
    edges[:, INNER:] = jnp.zeros((EDGE, RIM), bf16)
    for shift in range(BLOCKS):
        first = pl.multiple_of((lax.axis_index("rad") + shift) % BLOCKS * 256, 256)
        chunks[shift][...] = edges[:, pl.ds(first, 256)]
    copies[2 + PARTS].wait()

    row = lax.axis_index("ang") // 4
    panel, half = row // 4, (row // 2) % 2
    for r in range(GROUP):
        member, y = r // 4, r % 4
        served = (3 - 2 * half - member, 2 * half + 1 - member)
        wanted = []
        for m in range(2):
            tile = (4 * (1 - panel) + served[m]) * 4 + y
            listed = cells[0, pl.ds(tile, 1), :]
            wanted.append(jnp.where(iota((1, CAP), 1) < block_size[0, tile], listed, -1))
        wanted = jnp.concatenate(wanted, axis=1)
        hot = (iota((INNER, 2 * CAP), 0) == wanted).astype(f32).astype(bf16)
        lists[r] = dot(rounded[...], hot).astype(bf16)
        sends.append(pltpu.make_async_copy(lists.at[r], lists_hbm.at[r], sent.at[PARTS + r]))
        sends[-1].start()
    for copy in sends:
        copy.wait()


def setup_kernel(
    lower, upper, corner, block_inverse, slots, factors, needed, spikes, meta
):
    meta[:4, :] = slots[...].astype(f32)
    meta[4:, :] = factors[...]
    size = 2 * BLOCKS
    shape = (size, 128)
    row, lane = iota(shape, 0), iota(shape, 1)
    work = ((row == lane) | (row + size == lane)).astype(f32)
    for k in range(BLOCKS):
        for b in range(2):
            i = b * (DEPTH - 1)
            here = row == 2 * k + b
            if k < BLOCKS - 1:
                value = corner[k, i, DEPTH - 1] * upper[k]
                work = jnp.where(here & (lane == 2 * k + 2), value, work)
            if k > 0:
                value = corner[k, i, 0] * lower[k - 1]
                work = jnp.where(here & (lane == 2 * k - 1), value, work)
    for p in range(size):
        column = jnp.sum(jnp.where(lane == p, work, 0.0), axis=1, keepdims=True)
        chosen = work[p : p + 1, :] / column[p : p + 1, :]
        work = jnp.where(row == p, chosen, work - column * chosen)
    up = jnp.concatenate([work[2:, :], jnp.zeros((2, 128), f32)], axis=0)
    down = jnp.concatenate([jnp.zeros((2, 128), f32), work[:-2, :]], axis=0)
    needed[...] = jnp.where(row % 2 == 0, up, down)

    k = lax.axis_index("rad")
    ahead = jnp.where(k < BLOCKS - 1, upper[jnp.minimum(k, BLOCKS - 2)], 0.0)
    behind = jnp.where(k > 0, lower[jnp.maximum(k - 1, 0)], 0.0)
    rows = (iota((ROWS, DEPTH), 0) % DEPTH == iota((ROWS, DEPTH), 1)).astype(f32)
    tiled = jnp.dot(rows, block_inverse[k], precision=highest)
    right, left = tiled[:, DEPTH - 1 :] * ahead, tiled[:, :1] * behind
    channel, lane = iota((ROWS, 128), 0) // DEPTH, iota((ROWS, 128), 1)
    full = jnp.where(lane % 64 == channel, right, 0.0)
    full = full + jnp.where(lane % 64 == channel + 32, left, 0.0)
    high, low = split(full)
    spikes[...] = jnp.where(lane < 64, high.astype(f32), low.astype(f32)).astype(bf16)


def partial_kernel(first_meta, second_meta, lists, coupled, first, second, shared):
    base = lax.axis_index("ang") // GROUP * GROUP
    shared[:, :EDGE, :] = coupled[...]
    for m, (meta, partial) in enumerate(((first_meta, first), (second_meta, second))):
        slots = meta[:4, :].astype(jnp.int32) - base * CAP
        position = iota((GROUP * CAP, RIM), 0)
        weights = jnp.zeros((GROUP * CAP, RIM), f32)
        for d in range(4):
            hit = slots[d : d + 1, :] == position
            weights = weights + jnp.where(hit, meta[4 + d : 5 + d, :], 0.0)
        values = [lists[r, :, m * CAP : (m + 1) * CAP] for r in range(GROUP)]
        result = dot(jnp.concatenate(values, axis=1), weights.astype(bf16)).astype(bf16)
        partial[...] = result
        edges = dot(edge_select(ROWS, CHANNELS, 0), result).astype(bf16)
        for k in range(BLOCKS):
            shared[k, EDGE * (m + 1) : EDGE * (m + 2), :] = edges


def solve_kernel(needed, meta, *refs):
    chunks, coupled, passed = refs[:BLOCKS], refs[BLOCKS], refs[BLOCKS + 1]
    passed[...] = meta[...]
    values = [chunks[shift][...].astype(f32) for shift in range(BLOCKS)]
    for k in range(BLOCKS):
        for p in range(2):
            total = jnp.zeros((32, 256), f32)
            for shift in range(BLOCKS):
                block = (lax.axis_index("rad") + BLOCKS - shift) % BLOCKS
                for b in range(2):
                    factor = needed[2 * k + p, 2 * BLOCKS + 2 * block + b]
                    total = total + factor * values[shift][32 * b : 32 * b + 32, :]
            coupled[k, 32 * p : 32 * p + 32, :] = total.astype(bf16)


def own_kernel(needed, shared, *outs):
    own = lax.axis_index("rad")
    for m in range(2):
        for p in range(2):
            total = jnp.zeros((32, RIM), f32)
            for k in range(BLOCKS):
                for b in range(2):
                    factor = needed[2 * own + p, 2 * BLOCKS + 2 * k + b]
                    row = EDGE * (m + 1) + 32 * b
                    total = total + factor * shared[k, row : row + 32, :].astype(f32)
            outs[m][32 * p : 32 * p + 32, :] = total.astype(bf16)


def finish_kernel(spread, shared, spikes, result):
    for j in range(2):
        here = slice(256 * j, 256 * (j + 1))
        coupled = shared[j, :EDGE, :]
        correction = dot(spikes[...], jnp.concatenate([coupled, coupled], axis=0))
        result[:, here] = (spread[:, here] - correction).astype(bf16)


def ghost_kernel(whole, first, second, first_coupled, second_coupled, spikes, result):
    del whole
    high, low = split(first_coupled[...].astype(f32) + second_coupled[...].astype(f32))
    correction = dot(spikes[...], jnp.concatenate([high, high], axis=0))
    correction = correction + dot(spikes[:, :EDGE], low)
    ghost = first[...].astype(f32) + second[...].astype(f32)
    result[...] = (ghost - correction).astype(bf16)


SMEM = pl.BlockSpec(memory_space=pltpu.SMEM)
VMEM = pl.BlockSpec(memory_space=pltpu.VMEM)
ANY = pl.BlockSpec(memory_space=pl.ANY)


def whole(shape):
    return pl.BlockSpec(shape, lambda i: (0,) * len(shape))


def crossing(m, backwards):
    pairs = []
    for z in range(8):
        panel, i = divmod(z, 4)
        target = 4 * (1 - panel) + SERVES[m][i]
        for y in range(4):
            pair = (z * 4 + y, target * 4 + y)
            pairs.append(pair[::-1] if backwards else pair)
    return pairs


def shards(
    field,
    velocity,
    send_cells,
    block_size,
    donor_slot,
    intersection_weight,
    block_inverse,
    lower_coupling,
    upper_coupling,
):
    field = field.reshape(ROWS, CELLS)
    velocity = velocity.reshape(3 * DEPTH, CELLS)

    groups = [list(range(g * GROUP, (g + 1) * GROUP)) for g in range(TILES // GROUP)]
    spread, lists, *chunks = pl.pallas_call(
        head_kernel,
        in_specs=[SMEM] + [ANY] * 4,
        out_specs=[ANY] * 2 + [VMEM] * BLOCKS,
        out_shape=[
            jax.ShapeDtypeStruct((ROWS, CELLS), f32),
            jax.ShapeDtypeStruct((GROUP, ROWS, 2 * CAP), bf16),
        ]
        + [jax.ShapeDtypeStruct((EDGE, 256), bf16)] * BLOCKS,
        scratch_shapes=[
            pltpu.VMEM((1, TILES, CAP), jnp.int32),
            pltpu.VMEM((ROWS, CELLS), bf16),
            pltpu.VMEM((3 * DEPTH, CELLS), bf16),
            pltpu.VMEM((DEPTH, DEPTH), f32),
            pltpu.VMEM((ROWS, INNER), f32),
            pltpu.VMEM((ROWS, INNER), bf16),
            pltpu.VMEM((GROUP, ROWS, 2 * CAP), bf16),
            pltpu.VMEM((EDGE, CELLS), bf16),
            pltpu.SemaphoreType.DMA((3 + PARTS,)),
            pltpu.SemaphoreType.DMA((PARTS + GROUP,)),
        ],
        compiler_params=params(60),
        name="head",
    )(block_size, send_cells, field, velocity, block_inverse)

    donors = lax.all_to_all(lists, "ang", 0, 0, axis_index_groups=groups)
    chunks = chunks[:1] + [
        lax.ppermute(chunks[shift], "rad", [(k, (k + shift) % BLOCKS) for k in range(BLOCKS)])
        for shift in range(1, BLOCKS)
    ]

    needed, spikes, meta = pl.pallas_call(
        setup_kernel,
        in_specs=[SMEM] * 3 + [VMEM] * 3,
        out_specs=[VMEM] * 3,
        out_shape=[
            jax.ShapeDtypeStruct((2 * BLOCKS, 128), f32),
            jax.ShapeDtypeStruct((ROWS, 128), bf16),
            jax.ShapeDtypeStruct((8, RIM), f32),
        ],
        compiler_params=params(4),
        name="setup",
    )(
        lower_coupling,
        upper_coupling,
        block_inverse,
        block_inverse,
        donor_slot,
        intersection_weight,
    )

    coupled, meta = pl.pallas_call(
        solve_kernel,
        in_specs=[SMEM] + [VMEM] * (BLOCKS + 1),
        out_specs=[VMEM] * 2,
        out_shape=[
            jax.ShapeDtypeStruct((BLOCKS, EDGE, 256), bf16),
            jax.ShapeDtypeStruct((8, RIM), f32),
        ],
        compiler_params=params(4),
        name="solve",
    )(needed, meta, *chunks)

    metas = [lax.ppermute(meta, "ang", crossing(m, True)) for m in range(2)]
    first, second, shared = pl.pallas_call(
        partial_kernel,
        in_specs=[VMEM] * 4,
        out_specs=[VMEM] * 3,
        out_shape=[
            jax.ShapeDtypeStruct((ROWS, RIM), bf16),
            jax.ShapeDtypeStruct((ROWS, RIM), bf16),
            jax.ShapeDtypeStruct((BLOCKS, 3 * EDGE, 256), bf16),
        ],
        compiler_params=params(14),
        name="partial",
    )(*metas, donors, coupled)

    shared = lax.all_to_all(shared, "rad", 0, 0)
    ghosts = [lax.ppermute(value, "ang", crossing(m, False)) for m, value in enumerate((first, second))]

    own = pl.pallas_call(
        own_kernel,
        in_specs=[SMEM, VMEM],
        out_specs=[VMEM] * 2,
        out_shape=[jax.ShapeDtypeStruct((EDGE, RIM), bf16)] * 2,
        compiler_params=params(4),
        name="own",
    )(needed, shared)
    own = [lax.ppermute(value, "ang", crossing(m, False)) for m, value in enumerate(own)]

    result = pl.pallas_call(
        finish_kernel,
        grid=(CELLS // 512,),
        in_specs=[
            pl.BlockSpec((ROWS, 512), lambda i: (0, i)),
            pl.BlockSpec((2, 3 * EDGE, 256), lambda i: (i, 0, 0)),
            whole((ROWS, 128)),
        ],
        out_specs=pl.BlockSpec((ROWS, 512), lambda i: (0, i)),
        out_shape=jax.ShapeDtypeStruct((ROWS, CELLS), bf16),
        compiler_params=params(6),
        name="finish",
    )(spread, shared, spikes)

    result = pl.pallas_call(
        ghost_kernel,
        grid=(1,),
        in_specs=[ANY] + [whole((ROWS, RIM))] * 2 + [whole((EDGE, RIM))] * 2 + [whole((ROWS, 128))],
        out_specs=pl.BlockSpec((ROWS, RIM), lambda i: (0, INNER // RIM)),
        out_shape=jax.ShapeDtypeStruct((ROWS, CELLS), bf16),
        input_output_aliases={0: 0},
        compiler_params=params(6),
        name="ghosts",
    )(result, *ghosts, *own, spikes)
    return result.reshape(CHANNELS, DEPTH, CELLS)


def solution(mesh):
    in_specs = (
        P(None, "rad", "ang"),
        P(None, "rad", "ang"),
        P("ang", None, None),
        P("ang", None),
        P(None, "ang"),
        P(None, "ang"),
        P(),
        P(),
        P(),
    )
    out_specs = P(None, "rad", "ang")
    return jax.shard_map(shards, mesh=mesh, in_specs=in_specs, out_specs=out_specs, check_vma=False)
```

```python
import jax
import jax.numpy as jnp
from jax import lax
from jax.experimental import pallas as pl
from jax.experimental.pallas import tpu as pltpu
from jax.sharding import PartitionSpec as P

f32 = jnp.float32
bf16 = jnp.bfloat16
highest = lax.Precision.HIGHEST
induction = 0.5

CHANNELS = 27
DEPTH = 16
ROWS = CHANNELS * DEPTH
CELLS = 2048
RIM = 256
INNER = CELLS - RIM
CAP = 128
TILES = 32
BLOCKS = 8
PARTS = 3
PART_ROWS = ROWS // PARTS
EDGE = 64
GROUP = 8

SERVES = ((3, 2, 1, 0), (1, 0, 3, 2))


def params(mebibytes):
    return pltpu.CompilerParams(vmem_limit_bytes=mebibytes * 1024 * 1024)


def iota(shape, axis):
    return lax.broadcasted_iota(jnp.int32, shape, axis)


def split(value):
    high = value.astype(bf16)
    return high, (value - high.astype(f32)).astype(bf16)


def dot(left, right):
    return jnp.dot(left, right, preferred_element_type=f32)


def edge_select(rows, channels, first):
    row, column = iota((EDGE, rows), 0), iota((EDGE, rows), 1)
    channel = row % 32 - first
    wanted = channel * DEPTH + (row // 32) * (DEPTH - 1)
    return ((channel >= 0) & (channel < channels) & (column == wanted)).astype(f32).astype(bf16)


def head_kernel(block_size, cells_hbm, field_hbm, velocity_hbm, inverse_hbm, *refs):
    spread_hbm, lists_hbm, chunks = refs[0], refs[1], refs[2 : 2 + BLOCKS]
    cells, field, velocity, own, spread, rounded, lists, edges, done, sent = refs[2 + BLOCKS :]
    copies = [
        pltpu.make_async_copy(inverse_hbm.at[lax.axis_index("rad")], own, done.at[0]),
        pltpu.make_async_copy(velocity_hbm, velocity, done.at[1]),
    ]
    for part in range(PARTS):
        rows = pl.ds(part * PART_ROWS, PART_ROWS)
        copies.append(pltpu.make_async_copy(field_hbm.at[rows], field.at[rows], done.at[2 + part]))
    copies.append(pltpu.make_async_copy(cells_hbm, cells, done.at[2 + PARTS]))
    for copy in copies:
        copy.start()
    sends = []

    size = PART_ROWS
    rows = (iota((size, DEPTH), 0) % DEPTH == iota((size, DEPTH), 1)).astype(f32)
    columns = (iota((DEPTH, size), 1) % DEPTH == iota((DEPTH, size), 0)).astype(f32)
    same = iota((size, size), 0) // DEPTH == iota((size, size), 1) // DEPTH
    copies[0].wait()
    tiled = jnp.dot(jnp.dot(rows, own[...], precision=highest), columns, precision=highest)
    high_mat, low_mat = split(jnp.where(same, tiled, 0.0))
    matrix = jnp.concatenate([high_mat.astype(f32), high_mat.astype(f32), low_mat.astype(f32)], axis=1)
    matrix = matrix.astype(bf16)

    copies[1].wait()
    flow = [velocity[DEPTH * i : DEPTH * (i + 1), :INNER].astype(f32) for i in range(3)]
    for part in range(PARTS):
        copies[2 + part].wait()
        sources = []
        for m in range(PART_ROWS // (3 * DEPTH)):
            first = part * PART_ROWS + 3 * m * DEPTH
            f = [
                field[first + DEPTH * i : first + DEPTH * (i + 1), :INNER].astype(f32)
                for i in range(3)
            ]
            for i in range(3):
                j, k = (i + 1) % 3, (i + 2) % 3
                sources.append(f[i] + induction * (flow[j] * f[k] - flow[k] * f[j]))
        source_high, source_low = split(jnp.concatenate(sources, axis=0))
        result = dot(matrix, jnp.concatenate([source_high, source_low, source_high], axis=0))
        here = slice(part * PART_ROWS, (part + 1) * PART_ROWS)
        spread[here, :] = result
        rounded[here, :] = result.astype(bf16)
        rows = pl.ds(part * PART_ROWS, PART_ROWS)
        target = spread_hbm.at[rows, pl.ds(0, INNER)]
        sends.append(pltpu.make_async_copy(spread.at[rows], target, sent.at[part]))
        sends[-1].start()
    edges[:, :INNER] = dot(edge_select(ROWS, CHANNELS, 0), rounded[...]).astype(bf16)
    edges[:, INNER:] = jnp.zeros((EDGE, RIM), bf16)
    for shift in range(BLOCKS):
        first = pl.multiple_of((lax.axis_index("rad") + shift) % BLOCKS * 256, 256)
        chunks[shift][...] = edges[:, pl.ds(first, 256)]
    copies[2 + PARTS].wait()

    row = lax.axis_index("ang") // 4
    panel, half = row // 4, (row // 2) % 2
    for r in range(GROUP):
        member, y = r // 4, r % 4
        served = (3 - 2 * half - member, 2 * half + 1 - member)
        wanted = []
        for m in range(2):
            tile = (4 * (1 - panel) + served[m]) * 4 + y
            listed = cells[0, pl.ds(tile, 1), :]
            wanted.append(jnp.where(iota((1, CAP), 1) < block_size[0, tile], listed, -1))
        wanted = jnp.concatenate(wanted, axis=1)
        hot = (iota((INNER, 2 * CAP), 0) == wanted).astype(f32).astype(bf16)
        lists[r] = dot(rounded[...], hot).astype(bf16)
        sends.append(pltpu.make_async_copy(lists.at[r], lists_hbm.at[r], sent.at[PARTS + r]))
        sends[-1].start()
    for copy in sends:
        copy.wait()


def setup_kernel(
    lower, upper, corner, block_inverse, slots, factors, needed, spikes, meta
):
    meta[:4, :] = slots[...].astype(f32)
    meta[4:, :] = factors[...]
    size = 2 * BLOCKS
    shape = (size, 128)
    row, lane = iota(shape, 0), iota(shape, 1)
    work = ((row == lane) | (row + size == lane)).astype(f32)
    for k in range(BLOCKS):
        for b in range(2):
            i = b * (DEPTH - 1)
            here = row == 2 * k + b
            if k < BLOCKS - 1:
                value = corner[k, i, DEPTH - 1] * upper[k]
                work = jnp.where(here & (lane == 2 * k + 2), value, work)
            if k > 0:
                value = corner[k, i, 0] * lower[k - 1]
                work = jnp.where(here & (lane == 2 * k - 1), value, work)
    for p in range(size):
        column = jnp.sum(jnp.where(lane == p, work, 0.0), axis=1, keepdims=True)
        chosen = work[p : p + 1, :] / column[p : p + 1, :]
        work = jnp.where(row == p, chosen, work - column * chosen)
    up = jnp.concatenate([work[2:, :], jnp.zeros((2, 128), f32)], axis=0)
    down = jnp.concatenate([jnp.zeros((2, 128), f32), work[:-2, :]], axis=0)
    needed[...] = jnp.where(row % 2 == 0, up, down)

    k = lax.axis_index("rad")
    ahead = jnp.where(k < BLOCKS - 1, upper[jnp.minimum(k, BLOCKS - 2)], 0.0)
    behind = jnp.where(k > 0, lower[jnp.maximum(k - 1, 0)], 0.0)
    rows = (iota((ROWS, DEPTH), 0) % DEPTH == iota((ROWS, DEPTH), 1)).astype(f32)
    tiled = jnp.dot(rows, block_inverse[k], precision=highest)
    right, left = tiled[:, DEPTH - 1 :] * ahead, tiled[:, :1] * behind
    channel, lane = iota((ROWS, 128), 0) // DEPTH, iota((ROWS, 128), 1)
    full = jnp.where(lane % 64 == channel, right, 0.0)
    full = full + jnp.where(lane % 64 == channel + 32, left, 0.0)
    high, low = split(full)
    spikes[...] = jnp.where(lane < 64, high.astype(f32), low.astype(f32)).astype(bf16)


def partial_kernel(first_meta, second_meta, lists, coupled, first, second, shared):
    base = lax.axis_index("ang") // GROUP * GROUP
    shared[:, :EDGE, :] = coupled[...]
    for m, (meta, partial) in enumerate(((first_meta, first), (second_meta, second))):
        slots = meta[:4, :].astype(jnp.int32) - base * CAP
        position = iota((GROUP * CAP, RIM), 0)
        weights = jnp.zeros((GROUP * CAP, RIM), f32)
        for d in range(4):
            hit = slots[d : d + 1, :] == position
            weights = weights + jnp.where(hit, meta[4 + d : 5 + d, :], 0.0)
        values = [lists[r, :, m * CAP : (m + 1) * CAP] for r in range(GROUP)]
        result = dot(jnp.concatenate(values, axis=1), weights.astype(bf16)).astype(bf16)
        partial[...] = result
        edges = dot(edge_select(ROWS, CHANNELS, 0), result).astype(bf16)
        for k in range(BLOCKS):
            shared[k, EDGE * (m + 1) : EDGE * (m + 2), :] = edges


def solve_kernel(needed, meta, *refs):
    chunks, coupled, passed = refs[:BLOCKS], refs[BLOCKS], refs[BLOCKS + 1]
    passed[...] = meta[...]
    values = [chunks[shift][...].astype(f32) for shift in range(BLOCKS)]
    for k in range(BLOCKS):
        for p in range(2):
            total = jnp.zeros((32, 256), f32)
            for shift in range(BLOCKS):
                block = (lax.axis_index("rad") + BLOCKS - shift) % BLOCKS
                for b in range(2):
                    factor = needed[2 * k + p, 2 * BLOCKS + 2 * block + b]
                    total = total + factor * values[shift][32 * b : 32 * b + 32, :]
            coupled[k, 32 * p : 32 * p + 32, :] = total.astype(bf16)


def own_kernel(needed, shared, *outs):
    own = lax.axis_index("rad")
    for m in range(2):
        for p in range(2):
            total = jnp.zeros((32, RIM), f32)
            for k in range(BLOCKS):
                for b in range(2):
                    factor = needed[2 * own + p, 2 * BLOCKS + 2 * k + b]
                    row = EDGE * (m + 1) + 32 * b
                    total = total + factor * shared[k, row : row + 32, :].astype(f32)
            outs[m][32 * p : 32 * p + 32, :] = total.astype(bf16)


def finish_kernel(spread, shared, spikes, result):
    for j in range(INNER // 256):
        here = slice(256 * j, 256 * (j + 1))
        coupled = shared[j, :EDGE, :]
        correction = dot(spikes[...], jnp.concatenate([coupled, coupled], axis=0))
        result[:, here] = (spread[:, here] - correction).astype(bf16)
    result[:, INNER:] = jnp.zeros((PART_ROWS, RIM), bf16)


def ghost_kernel(whole, first, second, first_coupled, second_coupled, spikes, result):
    del whole
    high, low = split(first_coupled[...].astype(f32) + second_coupled[...].astype(f32))
    correction = dot(spikes[...], jnp.concatenate([high, high], axis=0))
    correction = correction + dot(spikes[:, :EDGE], low)
    ghost = first[...].astype(f32) + second[...].astype(f32)
    result[...] = (ghost - correction).astype(bf16)


SMEM = pl.BlockSpec(memory_space=pltpu.SMEM)
VMEM = pl.BlockSpec(memory_space=pltpu.VMEM)
ANY = pl.BlockSpec(memory_space=pl.ANY)


def whole(shape):
    return pl.BlockSpec(shape, lambda i: (0,) * len(shape))


def crossing(m, backwards):
    pairs = []
    for z in range(8):
        panel, i = divmod(z, 4)
        target = 4 * (1 - panel) + SERVES[m][i]
        for y in range(4):
            pair = (z * 4 + y, target * 4 + y)
            pairs.append(pair[::-1] if backwards else pair)
    return pairs


def shards(
    field,
    velocity,
    send_cells,
    block_size,
    donor_slot,
    intersection_weight,
    block_inverse,
    lower_coupling,
    upper_coupling,
):
    field = field.reshape(ROWS, CELLS)
    velocity = velocity.reshape(3 * DEPTH, CELLS)

    groups = [list(range(g * GROUP, (g + 1) * GROUP)) for g in range(TILES // GROUP)]
    spread, lists, *chunks = pl.pallas_call(
        head_kernel,
        in_specs=[SMEM] + [ANY] * 4,
        out_specs=[ANY] * 2 + [VMEM] * BLOCKS,
        out_shape=[
            jax.ShapeDtypeStruct((ROWS, CELLS), f32),
            jax.ShapeDtypeStruct((GROUP, ROWS, 2 * CAP), bf16),
        ]
        + [jax.ShapeDtypeStruct((EDGE, 256), bf16)] * BLOCKS,
        scratch_shapes=[
            pltpu.VMEM((1, TILES, CAP), jnp.int32),
            pltpu.VMEM((ROWS, CELLS), bf16),
            pltpu.VMEM((3 * DEPTH, CELLS), bf16),
            pltpu.VMEM((DEPTH, DEPTH), f32),
            pltpu.VMEM((ROWS, INNER), f32),
            pltpu.VMEM((ROWS, INNER), bf16),
            pltpu.VMEM((GROUP, ROWS, 2 * CAP), bf16),
            pltpu.VMEM((EDGE, CELLS), bf16),
            pltpu.SemaphoreType.DMA((3 + PARTS,)),
            pltpu.SemaphoreType.DMA((PARTS + GROUP,)),
        ],
        compiler_params=params(60),
        name="head",
    )(block_size, send_cells, field, velocity, block_inverse)

    donors = lax.all_to_all(lists, "ang", 0, 0, axis_index_groups=groups)
    chunks = chunks[:1] + [
        lax.ppermute(chunks[shift], "rad", [(k, (k + shift) % BLOCKS) for k in range(BLOCKS)])
        for shift in range(1, BLOCKS)
    ]

    needed, spikes, meta = pl.pallas_call(
        setup_kernel,
        in_specs=[SMEM] * 3 + [VMEM] * 3,
        out_specs=[VMEM] * 3,
        out_shape=[
            jax.ShapeDtypeStruct((2 * BLOCKS, 128), f32),
            jax.ShapeDtypeStruct((ROWS, 128), bf16),
            jax.ShapeDtypeStruct((8, RIM), f32),
        ],
        compiler_params=params(4),
        name="setup",
    )(
        lower_coupling,
        upper_coupling,
        block_inverse,
        block_inverse,
        donor_slot,
        intersection_weight,
    )

    coupled, meta = pl.pallas_call(
        solve_kernel,
        in_specs=[SMEM] + [VMEM] * (BLOCKS + 1),
        out_specs=[VMEM] * 2,
        out_shape=[
            jax.ShapeDtypeStruct((BLOCKS, EDGE, 256), bf16),
            jax.ShapeDtypeStruct((8, RIM), f32),
        ],
        compiler_params=params(4),
        name="solve",
    )(needed, meta, *chunks)

    metas = [lax.ppermute(meta, "ang", crossing(m, True)) for m in range(2)]
    first, second, shared = pl.pallas_call(
        partial_kernel,
        in_specs=[VMEM] * 4,
        out_specs=[VMEM] * 3,
        out_shape=[
            jax.ShapeDtypeStruct((ROWS, RIM), bf16),
            jax.ShapeDtypeStruct((ROWS, RIM), bf16),
            jax.ShapeDtypeStruct((BLOCKS, 3 * EDGE, 256), bf16),
        ],
        compiler_params=params(14),
        name="partial",
    )(*metas, donors, coupled)

    shared = lax.all_to_all(shared, "rad", 0, 0)
    ghosts = [lax.ppermute(value, "ang", crossing(m, False)) for m, value in enumerate((first, second))]

    own = pl.pallas_call(
        own_kernel,
        in_specs=[SMEM, VMEM],
        out_specs=[VMEM] * 2,
        out_shape=[jax.ShapeDtypeStruct((EDGE, RIM), bf16)] * 2,
        compiler_params=params(4),
        name="own",
    )(needed, shared)
    own = [lax.ppermute(value, "ang", crossing(m, False)) for m, value in enumerate(own)]

    result = pl.pallas_call(
        finish_kernel,
        grid=(PARTS,),
        in_specs=[
            pl.BlockSpec((PART_ROWS, CELLS), lambda i: (i, 0)),
            whole((BLOCKS, 3 * EDGE, 256)),
            pl.BlockSpec((PART_ROWS, 128), lambda i: (i, 0)),
        ],
        out_specs=pl.BlockSpec((PART_ROWS, CELLS), lambda i: (i, 0)),
        out_shape=jax.ShapeDtypeStruct((ROWS, CELLS), bf16),
        compiler_params=params(8),
        name="finish",
    )(spread, shared, spikes)

    result = pl.pallas_call(
        ghost_kernel,
        grid=(1,),
        in_specs=[ANY] + [whole((ROWS, RIM))] * 2 + [whole((EDGE, RIM))] * 2 + [whole((ROWS, 128))],
        out_specs=pl.BlockSpec((ROWS, RIM), lambda i: (0, INNER // RIM)),
        out_shape=jax.ShapeDtypeStruct((ROWS, CELLS), bf16),
        input_output_aliases={0: 0},
        compiler_params=params(6),
        name="ghosts",
    )(result, *ghosts, *own, spikes)
    return result.reshape(CHANNELS, DEPTH, CELLS)


def solution(mesh):
    in_specs = (
        P(None, "rad", "ang"),
        P(None, "rad", "ang"),
        P("ang", None, None),
        P("ang", None),
        P(None, "ang"),
        P(None, "ang"),
        P(),
        P(),
        P(),
    )
    out_specs = P(None, "rad", "ang")
    return jax.shard_map(shards, mesh=mesh, in_specs=in_specs, out_specs=out_specs, check_vma=False)
```
